32 devices in a mesh: seq: 8 (over z, x), ch: 4 (over y, core).
Axes of the slice: x: 2, y: 2, z: 4, core: 2. Of those that a mesh axis runs over, the one named last changes fastest.
Arguments:
- gate_rows: bfloat16 [4096, 2048], P(('seq', 'ch')), may hold values from -6 to 6
- key_rows: bfloat16 [4096, 2048], P(('seq', 'ch')), may hold values from -6 to 6
- value_rows: bfloat16 [4096, 2048], P(('seq', 'ch')), may hold values from -6 to 6
- spectrum: float32 [2, 16, 512, 2048], P(None, 'seq', None, 'ch'), may hold values from -6 to 6
- skip_bias: float32 [2048], replicated, may hold values from -1 to 1
Outputs:
- gated: bfloat16 [4096, 2048], P(('seq', 'ch'))
The draws below stay inside these ranges and needn't reach their ends.
All inputs are finite; a program needn't handle non-finite values.
Results may differ from the reference program's by a relative error of at most 0.0049.
Values may be sent and summed in bfloat16 or wider, within the bound.
No kernel may reach another device: no remote copies, remote signals or barrier semaphores. Data moves between devices by JAX's collectives and lax.ppermute only.
A program may use at most 128 MiB of HBM per device.

```python
import jax
import jax.numpy as jnp
from jax import lax

C = 2048
TOK_SEQ = 512
LENGTH = 4096
OFFSETS = 16


def shard_levels(key, dims, pieces, smallest, top_value):
    loudness = 1.0
    for axis_at, shards_of in pieces:
        heights = jax.random.uniform(jax.random.fold_in(jax.random.fold_in(key, 6), axis_at), (shards_of,), jnp.float32, smallest / len(pieces), top_value / len(pieces))
        loudness = loudness * jnp.repeat(jnp.exp(heights), dims[axis_at] // shards_of).reshape((-1,) + (1,) * (len(dims) - 1 - axis_at))
    return loudness


def scatter_about(stream_key, shape, scale, most, split=(), dtype=jnp.bfloat16):
    values = jax.random.normal(stream_key, shape, jnp.float32) * scale
    if len(split) > 0:
        values = shard_levels(stream_key, shape, split, -0.22, 0.18) * values
    return jnp.clip(values, min=-most, max=most).astype(dtype)


def setup_inputs(seed: int = 0) -> dict:
    arg_keys = jax.random.split(jax.random.key(seed), 6)
    gate_rows = scatter_about(arg_keys[0], (LENGTH, C), 1.0, 6.0, ((0, 32),))
    key_rows = scatter_about(arg_keys[1], (LENGTH, C), 1.0, 6.0, ((0, 32),))
    value_rows = scatter_about(arg_keys[2], (LENGTH, C), 1.0, 6.0, ((0, 32),))
    spectrum = scatter_about(arg_keys[3], (2, OFFSETS, TOK_SEQ, C), 1.0, 6.0, ((1, 8), (3, 4)), jnp.float32)
    skip_bias = jnp.clip(jax.random.uniform(arg_keys[4], (C,), jnp.float32, -1.0, 1.0), -1.0, 1.0)
    return dict(gate_rows=gate_rows, key_rows=key_rows, value_rows=value_rows, spectrum=spectrum, skip_bias=skip_bias)


def reference(gate_rows, key_rows, value_rows, spectrum, skip_bias):
    product = (key_rows.astype(jnp.float32) * value_rows.astype(jnp.float32)).astype(jnp.bfloat16)
    length_two = 2 * LENGTH
    spec_real = jnp.transpose(spectrum[0], (1, 0, 2)).reshape(length_two, C)
    spec_imag = jnp.transpose(spectrum[1], (1, 0, 2)).reshape(length_two, C)
    width = min(C, 128)
    count = C // width
    blocks_in = jnp.transpose(product.astype(jnp.float32).reshape(LENGTH, count, width), (1, 0, 2))
    blocks_re = jnp.transpose(spec_real.reshape(length_two, count, width), (1, 0, 2))
    blocks_im = jnp.transpose(spec_imag.reshape(length_two, count, width), (1, 0, 2))

    def one_block(items):
        signal, part_re, part_im = items
        transform = jnp.fft.fft(signal, n=length_two, axis=0)
        filtered = transform * (part_re + 1j * part_im)
        return jnp.real(jnp.fft.ifft(filtered, axis=0))[:LENGTH]

    fields = lax.map(one_block, (blocks_in, blocks_re, blocks_im))
    field = jnp.transpose(fields, (1, 0, 2)).reshape(LENGTH, C)
    gated = gate_rows.astype(jnp.float32) * (field + skip_bias[None, :] * product.astype(jnp.float32))
    return gated.astype(jnp.bfloat16)
```

```python
import functools
import math

import jax
import jax.numpy as jnp
import numpy as np
from jax import lax
from jax.experimental import pallas as pl
from jax.experimental.pallas import tpu as pltpu
from jax.sharding import PartitionSpec as P

highest = lax.Precision.HIGHEST
LANES = 128
MIB = 1 << 20


def phase_table(first, second, modulus):
    turns = first[:, None] * second[None, :] % modulus
    angles = turns.astype(jnp.float32) * (2.0 * math.pi / modulus)
    return (jnp.cos(angles), jnp.sin(angles))


def convolve(product, spectrum):
    seq_count = lax.axis_size("seq")
    tokens, width = product.shape
    length_two = 2 * seq_count * tokens
    offsets = jnp.arange(2 * seq_count, dtype=jnp.int32)
    places = jnp.arange(seq_count, dtype=jnp.int32)
    residues = jnp.arange(tokens, dtype=jnp.int32)
    off_cos, off_sin = phase_table(offsets, places, 2 * seq_count)
    res_cos, res_sin = phase_table(residues, residues, tokens)
    block = tokens // seq_count
    device = lax.axis_index("seq")
    pieces = lax.all_to_all(
        product.reshape(1, tokens, width), "seq", split_axis=1, concat_axis=0, tiled=True
    )
    values = pieces.astype(jnp.float32)
    real_part = jnp.einsum("kp,prc->krc", off_cos, values, precision=highest)
    imag_part = -jnp.einsum("kp,prc->krc", off_sin, values, precision=highest)
    own_rows = device * block + jnp.arange(block, dtype=jnp.int32)
    tw_cos, tw_sin = phase_table(offsets, own_rows, length_two)
    tw_cos = tw_cos[:, :, None]
    tw_sin = tw_sin[:, :, None]
    real_part, imag_part = (
        real_part * tw_cos + imag_part * tw_sin,
        imag_part * tw_cos - real_part * tw_sin,
    )
    real_part, imag_part = (
        lax.all_to_all(real_part, "seq", split_axis=0, concat_axis=1, tiled=True),
        lax.all_to_all(imag_part, "seq", split_axis=0, concat_axis=1, tiled=True),
    )
    real_next = jnp.einsum("grc,rs->gsc", real_part, res_cos, precision=highest) + jnp.einsum(
        "grc,rs->gsc", imag_part, res_sin, precision=highest
    )
    imag_next = jnp.einsum("grc,rs->gsc", imag_part, res_cos, precision=highest) - jnp.einsum(
        "grc,rs->gsc", real_part, res_sin, precision=highest
    )
    spec_real = spectrum[0]
    spec_imag = spectrum[1]
    real_part = real_next * spec_real - imag_next * spec_imag
    imag_part = real_next * spec_imag + imag_next * spec_real
    real_next = jnp.einsum("gsc,sr->grc", real_part, res_cos, precision=highest) - jnp.einsum(
        "gsc,sr->grc", imag_part, res_sin, precision=highest
    )
    imag_next = jnp.einsum("gsc,sr->grc", imag_part, res_cos, precision=highest) + jnp.einsum(
        "gsc,sr->grc", real_part, res_sin, precision=highest
    )
    own_offsets = 2 * device + jnp.arange(2, dtype=jnp.int32)
    un_cos, un_sin = phase_table(own_offsets, residues, length_two)
    un_cos = un_cos[:, :, None]
    un_sin = un_sin[:, :, None]
    real_part = real_next * un_cos - imag_next * un_sin
    imag_part = imag_next * un_cos + real_next * un_sin
    real_part, imag_part = (
        lax.all_to_all(real_part, "seq", split_axis=1, concat_axis=0, tiled=True),
        lax.all_to_all(imag_part, "seq", split_axis=1, concat_axis=0, tiled=True),
    )
    field = jnp.einsum("kp,krc->prc", off_cos, real_part, precision=highest) - jnp.einsum(
        "kp,krc->prc", off_sin, imag_part, precision=highest
    )
    field = field / length_two
    field = lax.all_to_all(field, "seq", split_axis=0, concat_axis=1, tiled=True)
    return field.reshape(tokens, width)


def any_mesh(gate_rows, key_rows, value_rows, spectrum, skip_bias):
    own = (key_rows.astype(jnp.float32) * value_rows.astype(jnp.float32)).astype(jnp.bfloat16)
    product = lax.all_to_all(own, "ch", split_axis=1, concat_axis=0, tiled=True)
    field = convolve(product, spectrum)
    field = lax.all_to_all(field, "ch", split_axis=0, concat_axis=1, tiled=True)
    gated = gate_rows.astype(jnp.float32) * (
        field + skip_bias[None, :] * own.astype(jnp.float32)
    )
    return gated.astype(jnp.bfloat16)


SEQ, CH, HALF = 8, 4, 4
VMEM = pl.BlockSpec(memory_space=pltpu.VMEM)
SMEM = pl.BlockSpec(memory_space=pltpu.SMEM)


def swap(array, axis, mask, count):
    return lax.ppermute(array, axis, [(i, i ^ mask) for i in range(count)])


def lanes_of(index, width):
    return pl.ds(pl.multiple_of(index * width, width), width)


def scatter_kernel(*refs):
    ins, outs = refs[:CH], refs[CH:]
    mine = lax.axis_index("ch")
    place = lax.axis_index("seq") % HALF
    rows = ins[0].shape[0]
    for from_ch in range(CH):
        at = pl.ds(pl.multiple_of((mine ^ from_ch) * rows, rows), rows)
        for member in range(HALF):
            outs[member][at, :] = ins[from_ch][:, lanes_of(place ^ member, LANES)]


def forward_kernel(*refs):
    blocks, (turn_ref, cos_ref, sin_ref, dft_ref, re_ref, im_ref, stage) = refs[:SEQ], refs[SEQ:]
    seq = lax.axis_index("seq")
    half, place = seq // HALF, seq % HALF
    size = blocks[0].shape[0]
    step = 32

    def rows_of(index, carry):
        at = pl.ds(pl.multiple_of(index * step, step), step)
        values = [ref[at, :].astype(jnp.float32) for ref in blocks]
        for member in range(HALF):
            for odd in range(2):
                j = 2 * (place ^ member) + odd
                residue = HALF * 2 * half + j
                real = imag = None
                for mask in range(SEQ):
                    turn = (residue * (seq ^ mask)) & (2 * SEQ - 1)
                    c, s = turn_ref[0, turn], turn_ref[1, turn]
                    real = values[mask] * c if real is None else real + values[mask] * c
                    imag = values[mask] * s if imag is None else imag + values[mask] * s
                cos, sin = cos_ref[j, at, :], sin_ref[j, at, :]
                out_re = (real * cos - imag * sin).astype(jnp.bfloat16)
                out_im = -(real * sin + imag * cos)
                to = pl.ds((2 * member + odd) * LANES, LANES)
                stage[at, to] = out_re
                stage[pl.ds(pl.multiple_of(size + index * step, step), step), to] = out_im.astype(jnp.bfloat16)
                stage[pl.ds(pl.multiple_of(2 * size + index * step, step), step), to] = -out_re
        return carry

    lax.fori_loop(0, size // step, rows_of, 0)
    for member in range(HALF):
        to = pl.ds(member * 2 * LANES, 2 * LANES)
        re_ref[:, to] = jnp.dot(dft_ref[...], stage[pl.ds(0, 2 * size), to], preferred_element_type=jnp.float32)
        im_ref[:, to] = jnp.dot(dft_ref[...], stage[pl.ds(size, 2 * size), to], preferred_element_type=jnp.float32)


def inverse_kernel(*refs):
    spec, (re_ref, im_ref, turn_ref, cos_ref, sin_ref, dft_ref) = refs[:HALF], refs[HALF : HALF + 6]
    outs, (stage, back_re, back_im) = refs[HALF + 6 : HALF + 6 + SEQ], refs[HALF + 6 + SEQ :]
    seq = lax.axis_index("seq")
    half, place = seq // HALF, seq % HALF
    size = re_ref.shape[0]
    step = 32
    for member in range(HALF):
        for odd in range(2):
            to = pl.ds((2 * member + odd) * LANES, LANES)
            x_re, x_im = re_ref[:, to], im_ref[:, to]
            h_re = spec[member][0, odd].astype(jnp.float32)
            h_im = spec[member][1, odd].astype(jnp.float32)
            y_re = (x_re * h_re - x_im * h_im).astype(jnp.bfloat16)
            y_im = (x_re * h_im + x_im * h_re).astype(jnp.bfloat16)
            stage[pl.ds(0, size), to] = y_im
            stage[pl.ds(size, size), to] = y_re
            stage[pl.ds(2 * size, size), to] = -y_im
        to = pl.ds(member * 2 * LANES, 2 * LANES)
        back_im[:, to] = jnp.dot(dft_ref[...], stage[pl.ds(0, 2 * size), to], preferred_element_type=jnp.float32)
        back_re[:, to] = jnp.dot(dft_ref[...], stage[pl.ds(size, 2 * size), to], preferred_element_type=jnp.float32)
    scale = 1.0 / (2 * SEQ * size)

    def rows_of(index, carry):
        at = pl.ds(pl.multiple_of(index * step, step), step)
        sums = [None] * SEQ
        for member in range(HALF):
            for odd in range(2):
                j = 2 * (place ^ member) + odd
                residue = HALF * 2 * half + j
                to = pl.ds((2 * member + odd) * LANES, LANES)
                cos, sin = cos_ref[j, at, :], sin_ref[j, at, :]
                real, imag = back_re[at, to], back_im[at, to]
                real, imag = real * cos - imag * sin, real * sin + imag * cos
                for mask in range(SEQ):
                    turn = (residue * (seq ^ mask)) & (2 * SEQ - 1)
                    term = real * turn_ref[0, turn] - imag * turn_ref[1, turn]
                    sums[mask] = term if sums[mask] is None else sums[mask] + term
        for mask in range(SEQ):
            outs[mask][at, :] = (sums[mask] * scale).astype(jnp.bfloat16)
        return carry

    lax.fori_loop(0, size // step, rows_of, 0)


def gather_kernel(*refs):
    ins, outs = refs[:SEQ], refs[SEQ:]
    mine = lax.axis_index("ch")
    place = lax.axis_index("seq") % HALF
    rows = outs[0].shape[0]
    for to_ch in range(CH):
        at = pl.ds(pl.multiple_of((mine ^ to_ch) * rows, rows), rows)
        for member in range(HALF):
            total = ins[member][at, :].astype(jnp.float32) + ins[member + HALF][at, :].astype(jnp.float32)
            outs[to_ch][:, lanes_of(place ^ member, LANES)] = total.astype(jnp.bfloat16)


def gate_kernel(gate_ref, key_ref, value_ref, skip_ref, *refs):
    fields, out_ref = refs[:CH], refs[CH]
    mine = lax.axis_index("ch")
    width = fields[0].shape[1]
    for from_ch in range(CH):
        at = lanes_of(mine ^ from_ch, width)
        product = (key_ref[:, at].astype(jnp.float32) * value_ref[:, at].astype(jnp.float32)).astype(jnp.bfloat16)
        field = fields[from_ch][...].astype(jnp.float32)
        gated = gate_ref[:, at].astype(jnp.float32) * (field + skip_ref[:, at] * product.astype(jnp.float32))
        out_ref[:, at] = gated.astype(jnp.bfloat16)


def call(kernel, name, ins, outs, scratch=(), limit=40 * MIB, flops=0, bytes_accessed=0):
    return pl.pallas_call(
        kernel,
        out_shape=tuple(jax.ShapeDtypeStruct(shape, dtype) for shape, dtype in outs),
        in_specs=[SMEM if x.shape == (2, 2 * SEQ) else VMEM for x in ins],
        out_specs=tuple(VMEM for _ in outs),
        scratch_shapes=list(scratch),
        compiler_params=pltpu.CompilerParams(vmem_limit_bytes=limit),
        cost_estimate=pl.CostEstimate(flops=flops, bytes_accessed=bytes_accessed, transcendentals=0),
        name=name,
    )(*ins)


def halves(gate_rows, key_rows, value_rows, spectrum, skip_bias):
    bf16, f32 = jnp.bfloat16, jnp.float32
    rows, channels = key_rows.shape
    size, width = rows * CH, channels // CH
    length_two = 2 * SEQ * size
    seq, ch = lax.axis_index("seq"), lax.axis_index("ch")
    half, place = seq // HALF, seq % HALF

    angles = np.arange(size)[:, None] * np.arange(size)[None, :] % size * (2.0 * np.pi / size)
    dft = jnp.asarray(np.concatenate([np.cos(angles), np.sin(angles)], axis=1), bf16)
    turns = np.arange(2 * SEQ) * (2.0 * np.pi / (2 * SEQ))
    turns = jnp.asarray(np.stack([np.cos(turns), np.sin(turns)]), f32)
    angles = np.arange(2 * SEQ)[:, None] * np.arange(size)[None, :] * (2.0 * np.pi / length_two)
    tables = []
    for part in (np.cos(angles), np.sin(angles)):
        part = lax.dynamic_slice_in_dim(jnp.asarray(part, f32), half * SEQ, SEQ, axis=0)
        tables.append(jnp.broadcast_to(part[:, :, None], (SEQ, size, LANES)))
    cos, sin = tables

    spec = [
        lax.dynamic_slice_in_dim(spectrum, (place ^ member) * LANES, LANES, axis=3).astype(bf16)
        for member in range(HALF)
    ]
    product = (key_rows.astype(f32) * value_rows.astype(f32)).astype(bf16)
    blocks = [lax.dynamic_slice_in_dim(product, (ch ^ mask) * width, width, axis=1) for mask in range(CH)]
    blocks = [blocks[0]] + [swap(blocks[mask], "ch", mask, CH) for mask in range(1, CH)]
    spec = [spec[0]] + [swap(spec[member], "seq", member, SEQ) for member in range(1, HALF)]

    sends = call(scatter_kernel, "rows_to_members", blocks, [((size, LANES), bf16)] * HALF)
    tokens = [sends[0]] + [swap(sends[mask % HALF], "seq", mask, SEQ) for mask in range(1, SEQ)]
    freq = call(
        forward_kernel,
        "forward",
        [*tokens, turns, cos, sin, dft],
        [((size, SEQ * LANES), f32)] * 2,
        [pltpu.VMEM((3 * size, SEQ * LANES), bf16)],
    )
    shares = call(
        inverse_kernel,
        "inverse",
        [*spec, *freq, turns, cos, sin, dft],
        [((size, LANES), bf16)] * SEQ,
        [pltpu.VMEM((3 * size, SEQ * LANES), bf16)] + [pltpu.VMEM((size, SEQ * LANES), f32)] * 2,
    )
    order = [0, 4, 5, 6, 7, 1, 2, 3]
    back = {mask: shares[mask] if mask == 0 else swap(shares[mask], "seq", mask, SEQ) for mask in order}
    rows_out = call(
        gather_kernel, "members_to_rows", [back[mask] for mask in range(SEQ)], [((rows, width), bf16)] * CH
    )
    fields = [rows_out[0]] + [swap(rows_out[mask], "ch", mask, CH) for mask in range(1, CH)]
    return call(
        gate_kernel,
        "gate",
        [gate_rows, key_rows, value_rows, skip_bias.reshape(1, channels), *fields],
        [((rows, channels), bf16)],
    )[0]


def solution(mesh):
    placed = (
        P(("seq", "ch"), None),
        P(("seq", "ch"), None),
        P(("seq", "ch"), None),
        P(None, "seq", None, "ch"),
        P(),
    )
    shape = dict(mesh.shape)
    body = halves if (shape["seq"], shape["ch"]) == (SEQ, CH) else any_mesh
    return jax.shard_map(
        body, mesh=mesh, in_specs=placed, out_specs=P(("seq", "ch"), None), check_vma=False
    )
```

```python
import functools
import math

import jax
import jax.numpy as jnp
import numpy as np
from jax import lax
from jax.experimental import pallas as pl
from jax.experimental.pallas import tpu as pltpu
from jax.sharding import PartitionSpec as P

highest = lax.Precision.HIGHEST
LANES = 128
MIB = 1 << 20


def phase_table(first, second, modulus):
    turns = first[:, None] * second[None, :] % modulus
    angles = turns.astype(jnp.float32) * (2.0 * math.pi / modulus)
    return (jnp.cos(angles), jnp.sin(angles))


def convolve(product, spectrum):
    seq_count = lax.axis_size("seq")
    tokens, width = product.shape
    length_two = 2 * seq_count * tokens
    offsets = jnp.arange(2 * seq_count, dtype=jnp.int32)
    places = jnp.arange(seq_count, dtype=jnp.int32)
    residues = jnp.arange(tokens, dtype=jnp.int32)
    off_cos, off_sin = phase_table(offsets, places, 2 * seq_count)
    res_cos, res_sin = phase_table(residues, residues, tokens)
    block = tokens // seq_count
    device = lax.axis_index("seq")
    pieces = lax.all_to_all(
        product.reshape(1, tokens, width), "seq", split_axis=1, concat_axis=0, tiled=True
    )
    values = pieces.astype(jnp.float32)
    real_part = jnp.einsum("kp,prc->krc", off_cos, values, precision=highest)
    imag_part = -jnp.einsum("kp,prc->krc", off_sin, values, precision=highest)
    own_rows = device * block + jnp.arange(block, dtype=jnp.int32)
    tw_cos, tw_sin = phase_table(offsets, own_rows, length_two)
    tw_cos = tw_cos[:, :, None]
    tw_sin = tw_sin[:, :, None]
    real_part, imag_part = (
        real_part * tw_cos + imag_part * tw_sin,
        imag_part * tw_cos - real_part * tw_sin,
    )
    real_part, imag_part = (
        lax.all_to_all(real_part, "seq", split_axis=0, concat_axis=1, tiled=True),
        lax.all_to_all(imag_part, "seq", split_axis=0, concat_axis=1, tiled=True),
    )
    real_next = jnp.einsum("grc,rs->gsc", real_part, res_cos, precision=highest) + jnp.einsum(
        "grc,rs->gsc", imag_part, res_sin, precision=highest
    )
    imag_next = jnp.einsum("grc,rs->gsc", imag_part, res_cos, precision=highest) - jnp.einsum(
        "grc,rs->gsc", real_part, res_sin, precision=highest
    )
    spec_real = spectrum[0]
    spec_imag = spectrum[1]
    real_part = real_next * spec_real - imag_next * spec_imag
    imag_part = real_next * spec_imag + imag_next * spec_real
    real_next = jnp.einsum("gsc,sr->grc", real_part, res_cos, precision=highest) - jnp.einsum(
        "gsc,sr->grc", imag_part, res_sin, precision=highest
    )
    imag_next = jnp.einsum("gsc,sr->grc", imag_part, res_cos, precision=highest) + jnp.einsum(
        "gsc,sr->grc", real_part, res_sin, precision=highest
    )
    own_offsets = 2 * device + jnp.arange(2, dtype=jnp.int32)
    un_cos, un_sin = phase_table(own_offsets, residues, length_two)
    un_cos = un_cos[:, :, None]
    un_sin = un_sin[:, :, None]
    real_part = real_next * un_cos - imag_next * un_sin
    imag_part = imag_next * un_cos + real_next * un_sin
    real_part, imag_part = (
        lax.all_to_all(real_part, "seq", split_axis=1, concat_axis=0, tiled=True),
        lax.all_to_all(imag_part, "seq", split_axis=1, concat_axis=0, tiled=True),
    )
    field = jnp.einsum("kp,krc->prc", off_cos, real_part, precision=highest) - jnp.einsum(
        "kp,krc->prc", off_sin, imag_part, precision=highest
    )
    field = field / length_two
    field = lax.all_to_all(field, "seq", split_axis=0, concat_axis=1, tiled=True)
    return field.reshape(tokens, width)


def any_mesh(gate_rows, key_rows, value_rows, spectrum, skip_bias):
    own = (key_rows.astype(jnp.float32) * value_rows.astype(jnp.float32)).astype(jnp.bfloat16)
    product = lax.all_to_all(own, "ch", split_axis=1, concat_axis=0, tiled=True)
    field = convolve(product, spectrum)
    field = lax.all_to_all(field, "ch", split_axis=0, concat_axis=1, tiled=True)
    gated = gate_rows.astype(jnp.float32) * (
        field + skip_bias[None, :] * own.astype(jnp.float32)
    )
    return gated.astype(jnp.bfloat16)


SEQ, CH, HALF = 8, 4, 4
DEVICES = SEQ * CH
ROOT = math.sqrt(0.5)
VMEM = pl.BlockSpec(memory_space=pltpu.VMEM)
STEP = 16


def swap(array, axis, mask, count):
    return lax.ppermute(array, axis, [(i, i ^ mask) for i in range(count)])


def columns_of(device):
    seq, ch = divmod(device, CH)
    return pl.ds((ch * HALF + seq % HALF) * LANES, LANES)


def rows_at(index, first=0):
    return pl.ds(pl.multiple_of(first + index * STEP, STEP), STEP)


def times(a, b):
    return a[0] * b[0] - a[1] * b[1], a[0] * b[1] + a[1] * b[0]


def root_16(power):
    return math.cos(power * math.pi / 8), math.sin(power * math.pi / 8)


def product_kernel(key_ref, value_ref, out_ref):
    for device in range(DEVICES // 2):
        at = columns_of(device)
        product = (key_ref[:, at].astype(jnp.float32) * value_ref[:, at].astype(jnp.float32)).astype(jnp.bfloat16)
        out_ref[device] = product
        out_ref[device + DEVICES // 2] = product


def four_real(a0, a1, a2, a3):
    even, odd = a0 + a2, a1 + a3
    less, more = (a1 - a3) * ROOT, odd * ROOT
    return (
        (even + odd, None),
        (a0 + less, -(a2 + more)),
        (a0 - a2, a3 - a1),
        (a0 - less, a2 - more),
        (even - odd, None),
    )


def residues_of(values, sign):
    even = four_real(*values[0::2])
    odd = four_real(*[v * sign for v in values[1::2]])
    out = [None] * SEQ
    out[0] = (even[0][0] + odd[0][0], None)
    out[4] = (even[4][0], -odd[4][0])
    for j in (1, 2, 3):
        turned = times(odd[j], root_16(-j))
        out[j] = (even[j][0] + turned[0], even[j][1] + turned[1])
        out[8 - j] = (even[j][0] - turned[0], turned[1] - even[j][1])
    return out


def four_back(zero, four, one, two, three):
    plus, minus = zero + four, zero - four
    half_way = (one[0] - three[0]) * ROOT
    across = (one[1] + three[1]) * ROOT
    return (
        plus + two[0] + (one[0] + three[0]),
        minus - two[1] + (half_way - across),
        plus - two[0] + (three[1] - one[1]),
        minus + two[1] - (half_way + across),
    )


def blocks_of(parts):
    sums, turned = [], []
    for j in (1, 2, 3):
        a, b = parts[j], parts[8 - j]
        sums.append((a[0] + b[0], a[1] - b[1]))
        turned.append(times((a[0] - b[0], a[1] + b[1]), root_16(j)))
    even = four_back(parts[0][0], parts[4][0], *sums)
    odd = four_back(parts[0][0], -parts[4][1], *turned)
    return [value for pair in zip(even, odd) for value in pair]


def sign_of_half():
    return jnp.where(lax.axis_index("seq") < HALF, 1.0, -1.0).astype(jnp.float32)


def twiddles(table, j):
    cos = jnp.broadcast_to(table[:, j : j + 1], (STEP, LANES))
    sin = jnp.broadcast_to(table[:, SEQ + j : SEQ + j + 1], (STEP, LANES))
    return cos, sin


def forward_kernel(tokens, table_ref, dft_ref, re_ref, im_ref, stage):
    half = lax.axis_index("seq") // HALF
    sign = sign_of_half()
    size = tokens.shape[1]

    def rows_of(index, carry):
        at = rows_at(index)
        table = table_ref[half, at, :]
        parts = residues_of([tokens[p, at, :].astype(jnp.float32) for p in range(SEQ)], sign)
        for j, (real, imag) in enumerate(parts):
            cos, sin = twiddles(table, j)
            if imag is None:
                real, imag = real * cos, -(real * sin)
            else:
                real, imag = real * cos + imag * sin, imag * cos - real * sin
            to = pl.ds(j * LANES, LANES)
            real = real.astype(jnp.bfloat16)
            stage[at, to] = real
            stage[rows_at(index, size), to] = imag.astype(jnp.bfloat16)
            stage[rows_at(index, 2 * size), to] = -real
        return carry

    lax.fori_loop(0, size // STEP, rows_of, 0)
    for pair in range(HALF):
        to = pl.ds(pair * 2 * LANES, 2 * LANES)
        re_ref[:, to] = jnp.dot(dft_ref[...], stage[pl.ds(0, 2 * size), to], preferred_element_type=jnp.float32)
        im_ref[:, to] = jnp.dot(dft_ref[...], stage[pl.ds(size, 2 * size), to], preferred_element_type=jnp.float32)


def inverse_kernel(*refs):
    spec, (re_ref, im_ref, table_ref, dft_ref, out_ref, stage, back_re, back_im) = refs[:HALF], refs[HALF:]
    seq = lax.axis_index("seq")
    half, place = seq // HALF, seq % HALF
    sign = sign_of_half()
    size = re_ref.shape[0]
    for member in range(HALF):
        for odd in range(2):
            to = pl.ds(pl.multiple_of((2 * (place ^ member) + odd) * LANES, LANES), LANES)
            x = re_ref[:, to], im_ref[:, to]
            h = spec[member][0, odd].astype(jnp.float32), spec[member][1, odd].astype(jnp.float32)
            y_re, y_im = times(x, h)
            y_re, y_im = y_re.astype(jnp.bfloat16), y_im.astype(jnp.bfloat16)
            to = pl.ds((2 * member + odd) * LANES, LANES)
            stage[pl.ds(0, size), to] = y_im
            stage[pl.ds(size, size), to] = y_re
            stage[pl.ds(2 * size, size), to] = -y_im
        to = pl.ds(member * 2 * LANES, 2 * LANES)
        into = pl.ds(pl.multiple_of((place ^ member) * 2 * LANES, 2 * LANES), 2 * LANES)
        back_im[:, into] = jnp.dot(dft_ref[...], stage[pl.ds(0, 2 * size), to], preferred_element_type=jnp.float32)
        back_re[:, into] = jnp.dot(dft_ref[...], stage[pl.ds(size, 2 * size), to], preferred_element_type=jnp.float32)
    scale = 1.0 / (2 * SEQ * size)

    def rows_of(index, carry):
        at = rows_at(index)
        table = table_ref[half, at, :]
        parts = []
        for j in range(SEQ):
            to = pl.ds(j * LANES, LANES)
            parts.append(times((back_re[at, to], back_im[at, to]), twiddles(table, j)))
        for p, value in enumerate(blocks_of(parts)):
            out_ref[p, at, :] = (value * (scale * sign if p % 2 else scale)).astype(jnp.bfloat16)
        return carry

    lax.fori_loop(0, size // STEP, rows_of, 0)


def gate_kernel(gate_ref, key_ref, value_ref, skip_ref, field_ref, out_ref):
    for device in range(DEVICES // 2):
        at = columns_of(device)
        product = (key_ref[:, at].astype(jnp.float32) * value_ref[:, at].astype(jnp.float32)).astype(jnp.bfloat16)
        field = field_ref[device].astype(jnp.float32) + field_ref[device + DEVICES // 2].astype(jnp.float32)
        gated = gate_ref[:, at].astype(jnp.float32) * (field + skip_ref[:, at] * product.astype(jnp.float32))
        out_ref[:, at] = gated.astype(jnp.bfloat16)


def call(kernel, name, ins, outs, scratch=(), limit=40 * MIB):
    return pl.pallas_call(
        kernel,
        out_shape=tuple(jax.ShapeDtypeStruct(shape, dtype) for shape, dtype in outs),
        in_specs=[VMEM for _ in ins],
        out_specs=tuple(VMEM for _ in outs),
        scratch_shapes=list(scratch),
        compiler_params=pltpu.CompilerParams(vmem_limit_bytes=limit),
        name=name,
    )(*ins)


def halves(gate_rows, key_rows, value_rows, spectrum, skip_bias):
    bf16, f32 = jnp.bfloat16, jnp.float32
    rows, channels = key_rows.shape
    size = rows * CH
    length_two = 2 * SEQ * size
    everywhere = ("seq", "ch")
    place = lax.axis_index("seq") % HALF

    angles = np.arange(size)[:, None] * np.arange(size)[None, :] % size * (2.0 * np.pi / size)
    dft = jnp.asarray(np.concatenate([np.cos(angles), np.sin(angles)], axis=1), bf16)
    angles = np.arange(size)[:, None] * np.arange(2 * SEQ)[None, :] * (2.0 * np.pi / length_two)
    table = np.stack([np.cos(angles), np.sin(angles)], axis=1).reshape(size, 2, 2, SEQ)
    table = jnp.asarray(table.transpose(2, 0, 1, 3).reshape(2, size, 2 * SEQ), f32)

    spec = [
        lax.dynamic_slice_in_dim(spectrum, (place ^ member) * LANES, LANES, axis=3).astype(bf16)
        for member in range(HALF)
    ]
    sends = call(product_kernel, "product", [key_rows, value_rows], [((DEVICES, rows, LANES), bf16)])[0]
    tokens = lax.all_to_all(sends, everywhere, split_axis=0, concat_axis=0, tiled=True).reshape(SEQ, size, LANES)
    spec = [spec[0]] + [swap(spec[member], "seq", member, SEQ) for member in range(1, HALF)]
    freq = call(
        forward_kernel,
        "forward",
        [tokens, table, dft],
        [((size, SEQ * LANES), f32)] * 2,
        [pltpu.VMEM((3 * size, SEQ * LANES), bf16)],
    )
    shares = call(
        inverse_kernel,
        "inverse",
        [*spec, *freq, table, dft],
        [((SEQ, size, LANES), bf16)],
        [pltpu.VMEM((3 * size, SEQ * LANES), bf16)] + [pltpu.VMEM((size, SEQ * LANES), f32)] * 2,
    )[0].reshape(DEVICES, rows, LANES)
    field = lax.all_to_all(shares, everywhere, split_axis=0, concat_axis=0, tiled=True)
    return call(
        gate_kernel,
        "gate",
        [gate_rows, key_rows, value_rows, skip_bias.reshape(1, channels), field],
        [((rows, channels), bf16)],
    )[0]


def solution(mesh):
    placed = (
        P(("seq", "ch"), None),
        P(("seq", "ch"), None),
        P(("seq", "ch"), None),
        P(None, "seq", None, "ch"),
        P(),
    )
    shape = dict(mesh.shape)
    body = halves if (shape["seq"], shape["ch"]) == (SEQ, CH) else any_mesh
    return jax.shard_map(
        body, mesh=mesh, in_specs=placed, out_specs=P(("seq", "ch"), None), check_vma=False
    )
```

```python
import functools
import math

import jax
import jax.numpy as jnp
import numpy as np
from jax import lax
from jax.experimental import pallas as pl
from jax.experimental.pallas import tpu as pltpu
from jax.sharding import PartitionSpec as P

highest = lax.Precision.HIGHEST
LANES = 128
MIB = 1 << 20


def phase_table(first, second, modulus):
    turns = first[:, None] * second[None, :] % modulus
    angles = turns.astype(jnp.float32) * (2.0 * math.pi / modulus)
    return (jnp.cos(angles), jnp.sin(angles))


def convolve(product, spectrum):
    seq_count = lax.axis_size("seq")
    tokens, width = product.shape
    length_two = 2 * seq_count * tokens
    offsets = jnp.arange(2 * seq_count, dtype=jnp.int32)
    places = jnp.arange(seq_count, dtype=jnp.int32)
    residues = jnp.arange(tokens, dtype=jnp.int32)
    off_cos, off_sin = phase_table(offsets, places, 2 * seq_count)
    res_cos, res_sin = phase_table(residues, residues, tokens)
    block = tokens // seq_count
    device = lax.axis_index("seq")
    pieces = lax.all_to_all(
        product.reshape(1, tokens, width), "seq", split_axis=1, concat_axis=0, tiled=True
    )
    values = pieces.astype(jnp.float32)
    real_part = jnp.einsum("kp,prc->krc", off_cos, values, precision=highest)
    imag_part = -jnp.einsum("kp,prc->krc", off_sin, values, precision=highest)
    own_rows = device * block + jnp.arange(block, dtype=jnp.int32)
    tw_cos, tw_sin = phase_table(offsets, own_rows, length_two)
    tw_cos = tw_cos[:, :, None]
    tw_sin = tw_sin[:, :, None]
    real_part, imag_part = (
        real_part * tw_cos + imag_part * tw_sin,
        imag_part * tw_cos - real_part * tw_sin,
    )
    real_part, imag_part = (
        lax.all_to_all(real_part, "seq", split_axis=0, concat_axis=1, tiled=True),
        lax.all_to_all(imag_part, "seq", split_axis=0, concat_axis=1, tiled=True),
    )
    real_next = jnp.einsum("grc,rs->gsc", real_part, res_cos, precision=highest) + jnp.einsum(
        "grc,rs->gsc", imag_part, res_sin, precision=highest
    )
    imag_next = jnp.einsum("grc,rs->gsc", imag_part, res_cos, precision=highest) - jnp.einsum(
        "grc,rs->gsc", real_part, res_sin, precision=highest
    )
    spec_real = spectrum[0]
    spec_imag = spectrum[1]
    real_part = real_next * spec_real - imag_next * spec_imag
    imag_part = real_next * spec_imag + imag_next * spec_real
    real_next = jnp.einsum("gsc,sr->grc", real_part, res_cos, precision=highest) - jnp.einsum(
        "gsc,sr->grc", imag_part, res_sin, precision=highest
    )
    imag_next = jnp.einsum("gsc,sr->grc", imag_part, res_cos, precision=highest) + jnp.einsum(
        "gsc,sr->grc", real_part, res_sin, precision=highest
    )
    own_offsets = 2 * device + jnp.arange(2, dtype=jnp.int32)
    un_cos, un_sin = phase_table(own_offsets, residues, length_two)
    un_cos = un_cos[:, :, None]
    un_sin = un_sin[:, :, None]
    real_part = real_next * un_cos - imag_next * un_sin
    imag_part = imag_next * un_cos + real_next * un_sin
    real_part, imag_part = (
        lax.all_to_all(real_part, "seq", split_axis=1, concat_axis=0, tiled=True),
        lax.all_to_all(imag_part, "seq", split_axis=1, concat_axis=0, tiled=True),
    )
    field = jnp.einsum("kp,krc->prc", off_cos, real_part, precision=highest) - jnp.einsum(
        "kp,krc->prc", off_sin, imag_part, precision=highest
    )
    field = field / length_two
    field = lax.all_to_all(field, "seq", split_axis=0, concat_axis=1, tiled=True)
    return field.reshape(tokens, width)


def any_mesh(gate_rows, key_rows, value_rows, spectrum, skip_bias):
    own = (key_rows.astype(jnp.float32) * value_rows.astype(jnp.float32)).astype(jnp.bfloat16)
    product = lax.all_to_all(own, "ch", split_axis=1, concat_axis=0, tiled=True)
    field = convolve(product, spectrum)
    field = lax.all_to_all(field, "ch", split_axis=0, concat_axis=1, tiled=True)
    gated = gate_rows.astype(jnp.float32) * (
        field + skip_bias[None, :] * own.astype(jnp.float32)
    )
    return gated.astype(jnp.bfloat16)


SEQ, CH, HALF = 8, 4, 4
DEVICES = SEQ * CH
ROOT = math.sqrt(0.5)
EARLY, LATE = (0, 1, 2), (3,)
VMEM = pl.BlockSpec(memory_space=pltpu.VMEM)
STEP = 16


def swap(array, axis, mask, count):
    return lax.ppermute(array, axis, [(i, i ^ mask) for i in range(count)])


def columns_of(device):
    seq, ch = divmod(device, CH)
    return pl.ds((ch * HALF + seq % HALF) * LANES, LANES)


def rows_at(index, first=0):
    return pl.ds(pl.multiple_of(first + index * STEP, STEP), STEP)


def times(a, b):
    return a[0] * b[0] - a[1] * b[1], a[0] * b[1] + a[1] * b[0]


def root_16(power):
    return math.cos(power * math.pi / 8), math.sin(power * math.pi / 8)


def product_kernel(key_hbm, value_hbm, out_ref, key, value, sems):
    groups = DEVICES // 2
    width = key.shape[1] // CH
    copies = []
    for ch in range(CH):
        at = pl.ds(ch * width, width)
        copies.append(
            [
                pltpu.make_async_copy(source.at[:, at], to.at[:, at], sems.at[which, ch])
                for which, (source, to) in enumerate(((key_hbm, key), (value_hbm, value)))
            ]
        )
        for copy in copies[-1]:
            copy.start()
    for ch in range(CH):
        for copy in copies[ch]:
            copy.wait()
        for member in range(HALF):
            device = member * CH + ch
            at = columns_of(device)
            product = (key[:, at].astype(jnp.float32) * value[:, at].astype(jnp.float32)).astype(jnp.bfloat16)
            out_ref[device] = product
            out_ref[device + groups] = product


def spectrum_kernel(place_ref, *refs):
    spec, members = refs[:HALF], refs[HALF:]
    rows = members[0].shape[3]
    for member in range(HALF):
        for part in range(2):
            for odd in range(2):
                for bit in range(2):
                    values = spec[member][part, odd, pl.ds(bit, rows, stride=2), :]
                    members[member][part, odd, bit] = values.astype(jnp.bfloat16)


def members_of(spectrum, steps=4):
    size = spectrum.shape[2]
    piece = size // steps
    place = (lax.axis_index("seq") % HALF).astype(jnp.int32).reshape(1)
    spec_blocks = [
        pl.BlockSpec((2, 2, piece, LANES), lambda i, place, member=member: (0, 0, i, place[0] ^ member))
        for member in range(HALF)
    ]
    return pl.pallas_call(
        spectrum_kernel,
        grid_spec=pltpu.PrefetchScalarGridSpec(
            num_scalar_prefetch=1,
            grid=(steps,),
            in_specs=spec_blocks,
            out_specs=[pl.BlockSpec((2, 2, 2, piece // 2, LANES), lambda i, place: (0, 0, 0, i, 0))] * HALF,
        ),
        out_shape=[jax.ShapeDtypeStruct((2, 2, 2, size // 2, LANES), jnp.bfloat16)] * HALF,
        compiler_params=pltpu.CompilerParams(vmem_limit_bytes=56 * MIB),
        name="spectrum",
    )(place, *[spectrum] * HALF)


def four_real(a0, a1, a2, a3):
    even, odd = a0 + a2, a1 + a3
    less, more = (a1 - a3) * ROOT, odd * ROOT
    return (
        (even + odd, None),
        (a0 + less, -(a2 + more)),
        (a0 - a2, a3 - a1),
        (a0 - less, a2 - more),
        (even - odd, None),
    )


def residues_of(values, sign):
    even = four_real(*values[0::2])
    odd = four_real(*[v * sign for v in values[1::2]])
    out = [None] * SEQ
    out[0] = (even[0][0] + odd[0][0], None)
    out[4] = (even[4][0], -odd[4][0])
    for j in (1, 2, 3):
        turned = times(odd[j], root_16(-j))
        out[j] = (even[j][0] + turned[0], even[j][1] + turned[1])
        out[8 - j] = (even[j][0] - turned[0], turned[1] - even[j][1])
    return out


def four_back(zero, four, one, two, three):
    plus, minus = zero + four, zero - four
    half_way = (one[0] - three[0]) * ROOT
    across = (one[1] + three[1]) * ROOT
    return (
        plus + two[0] + (one[0] + three[0]),
        minus - two[1] + (half_way - across),
        plus - two[0] + (three[1] - one[1]),
        minus + two[1] - (half_way + across),
    )


def blocks_of(parts):
    sums, turned = [], []
    for j in (1, 2, 3):
        a, b = parts[j], parts[8 - j]
        sums.append((a[0] + b[0], a[1] - b[1]))
        turned.append(times((a[0] - b[0], a[1] + b[1]), root_16(j)))
    even = four_back(parts[0][0], parts[4][0], *sums)
    odd = four_back(parts[0][0], -parts[4][1], *turned)
    return [value for pair in zip(even, odd) for value in pair]


def sign_of_half():
    return jnp.where(lax.axis_index("seq") < HALF, 1.0, -1.0).astype(jnp.float32)


def turn_table(size):
    angles = np.arange(2 * SEQ)[:, None] * np.arange(size)[None, :] * (2.0 * np.pi / (2 * SEQ * size))
    angles = angles.reshape(2, SEQ, size)
    between = np.broadcast_to(np.arange(size) * (2.0 * np.pi / size), (2, 1, size))
    angles = np.concatenate([angles, between], axis=1)
    table = np.stack([np.cos(angles), np.sin(angles)], axis=2).astype(np.float32)
    return jnp.asarray(np.repeat(table[..., None], LANES, axis=-1))


def forward_kernel(tokens, table, dft_ref, re_ref, im_ref, stage):
    sign = sign_of_half()
    size = tokens.shape[1]
    short = size // 2

    def rows_of(index, carry):
        both = []
        for first in (0, short):
            at = rows_at(index, first)
            parts = residues_of([tokens[p, at, :].astype(jnp.float32) for p in range(SEQ)], sign)
            turned = []
            for j, (real, imag) in enumerate(parts):
                cos, sin = table[j, 0, at, :], table[j, 1, at, :]
                if imag is None:
                    turned.append((real * cos, -(real * sin)))
                else:
                    turned.append((real * cos + imag * sin, imag * cos - real * sin))
            both.append(turned)
        at = rows_at(index)
        cos, sin = table[SEQ, 0, at, :], table[SEQ, 1, at, :]
        for j in range(SEQ):
            a, b = both[0][j], both[1][j]
            less = a[0] - b[0], a[1] - b[1]
            pair = (a[0] + b[0], a[1] + b[1]), (less[0] * cos + less[1] * sin, less[1] * cos - less[0] * sin)
            for bit, (real, imag) in enumerate(pair):
                to = pl.ds((bit * SEQ + j) * LANES, LANES)
                real = real.astype(jnp.bfloat16)
                stage[at, to] = real
                stage[rows_at(index, short), to] = imag.astype(jnp.bfloat16)
                stage[rows_at(index, size), to] = -real
        return carry

    lax.fori_loop(0, short // STEP, rows_of, 0)
    re_ref[...] = jnp.dot(dft_ref[...], stage[pl.ds(0, size), :], preferred_element_type=jnp.float32)
    im_ref[...] = jnp.dot(dft_ref[...], stage[pl.ds(short, size), :], preferred_element_type=jnp.float32)


def filter_members(members, spec, re_ref, im_ref, dft_ref, back_re, back_im, stage):
    place = lax.axis_index("seq") % HALF
    short = re_ref.shape[0]
    size = 2 * short
    for index, member in enumerate(members):
        for odd in range(2):
            for bit in range(2):
                column = bit * SEQ + 2 * (place ^ member) + odd
                at = pl.ds(pl.multiple_of(column * LANES, LANES), LANES)
                h = spec[index][0, odd, bit].astype(jnp.float32), spec[index][1, odd, bit].astype(jnp.float32)
                y_re, y_im = times((re_ref[:, at], im_ref[:, at]), h)
                y_re, y_im = y_re.astype(jnp.bfloat16), y_im.astype(jnp.bfloat16)
                to = pl.ds((odd * 2 + bit) * LANES, LANES)
                stage[index, pl.ds(0, short), to] = y_im
                stage[index, pl.ds(short, short), to] = y_re
                stage[index, pl.ds(size, short), to] = -y_im
        back_im[place ^ member] = jnp.dot(
            dft_ref[...], stage[index, pl.ds(0, size), :], preferred_element_type=jnp.float32
        )
        back_re[place ^ member] = jnp.dot(
            dft_ref[...], stage[index, pl.ds(short, size), :], preferred_element_type=jnp.float32
        )


def early_kernel(*refs):
    spec, (re_ref, im_ref, dft_ref, back_re, back_im, stage) = refs[: len(EARLY)], refs[len(EARLY) :]
    filter_members(EARLY, spec, re_ref, im_ref, dft_ref, back_re, back_im, stage)


def late_kernel(*refs):
    spec, refs = refs[: len(LATE)], refs[len(LATE) :]
    early_re, early_im, re_ref, im_ref, table, dft_ref, out_ref, back_re, back_im, stage = refs
    sign = sign_of_half()
    place = lax.axis_index("seq") % HALF
    short = re_ref.shape[0]
    size = 2 * short
    filter_members(LATE, spec, re_ref, im_ref, dft_ref, back_re, back_im, stage)
    for member in EARLY:
        back_re[place ^ member] = early_re[place ^ member]
        back_im[place ^ member] = early_im[place ^ member]
    scale = 1.0 / (2 * SEQ * size)

    def rows_of(index, carry):
        at = rows_at(index)
        late = rows_at(index, short)
        cos, sin = table[SEQ, 0, at, :], table[SEQ, 1, at, :]
        parts = [], []
        for j in range(SEQ):
            pair = []
            for bit in range(2):
                to = pl.ds((j % 2 * 2 + bit) * LANES, LANES)
                pair.append((back_re[j // 2, at, to], back_im[j // 2, at, to]))
            a, b = pair[0], times(pair[1], (cos, sin))
            parts[0].append(times((a[0] + b[0], a[1] + b[1]), (table[j, 0, at, :], table[j, 1, at, :])))
            parts[1].append(times((a[0] - b[0], a[1] - b[1]), (table[j, 0, late, :], table[j, 1, late, :])))
        for where, values in zip((at, late), parts):
            for p, value in enumerate(blocks_of(values)):
                out_ref[p, where, :] = (value * (scale * sign if p % 2 else scale)).astype(jnp.bfloat16)
        return carry

    lax.fori_loop(0, short // STEP, rows_of, 0)


def gate_kernel(gate_ref, key_ref, value_ref, skip_ref, field_ref, out_ref):
    for device in range(DEVICES // 2):
        at = columns_of(device)
        product = (key_ref[:, at].astype(jnp.float32) * value_ref[:, at].astype(jnp.float32)).astype(jnp.bfloat16)
        field = field_ref[device].astype(jnp.float32) + field_ref[device + DEVICES // 2].astype(jnp.float32)
        gated = gate_ref[:, at].astype(jnp.float32) * (field + skip_ref[:, at] * product.astype(jnp.float32))
        out_ref[:, at] = gated.astype(jnp.bfloat16)


def call(kernel, name, ins, outs, scratch=(), limit=24 * MIB, hbm=()):
    return pl.pallas_call(
        kernel,
        out_shape=tuple(jax.ShapeDtypeStruct(shape, dtype) for shape, dtype in outs),
        in_specs=[pl.BlockSpec(memory_space=pl.ANY) if index in hbm else VMEM for index, _ in enumerate(ins)],
        out_specs=tuple(VMEM for _ in outs),
        scratch_shapes=list(scratch),
        compiler_params=pltpu.CompilerParams(vmem_limit_bytes=limit),
        name=name,
    )(*ins)


def halves(gate_rows, key_rows, value_rows, spectrum, skip_bias):
    bf16, f32 = jnp.bfloat16, jnp.float32
    rows, channels = key_rows.shape
    size = rows * CH
    short = size // 2
    everywhere = ("seq", "ch")

    angles = np.arange(short)[:, None] * np.arange(short)[None, :] % short * (2.0 * np.pi / short)
    dft = jnp.asarray(np.concatenate([np.cos(angles), np.sin(angles)], axis=1), bf16)
    table = lax.dynamic_index_in_dim(turn_table(size), lax.axis_index("seq") // HALF, 0, keepdims=False)

    sends = call(
        product_kernel,
        "product",
        [key_rows, value_rows],
        [((DEVICES, rows, LANES), bf16)],
        [pltpu.VMEM((rows, channels), bf16)] * 2 + [pltpu.SemaphoreType.DMA((2, CH))],
        limit=56 * MIB,
        hbm=(0, 1),
    )[0]
    spec, table = lax.optimization_barrier((members_of(spectrum), table))
    tokens = lax.all_to_all(sends, everywhere, split_axis=0, concat_axis=0, tiled=True).reshape(SEQ, size, LANES)
    spec = [spec[0]] + [swap(spec[member], "seq", member, SEQ) for member in range(1, HALF)]
    freq = call(
        forward_kernel,
        "forward",
        [tokens, table, dft],
        [((short, 2 * SEQ * LANES), f32)] * 2,
        [pltpu.VMEM((3 * short, 2 * SEQ * LANES), bf16)],
    )
    back = ((HALF, short, 4 * LANES), f32)
    early = call(
        early_kernel,
        "early_members",
        [*[spec[member] for member in EARLY], *freq, dft],
        [back] * 2,
        [pltpu.VMEM((len(EARLY), 3 * short, 4 * LANES), bf16)],
    )
    shares = call(
        late_kernel,
        "late_member",
        [*[spec[member] for member in LATE], *early, *freq, table, dft],
        [((SEQ, size, LANES), bf16)],
        [pltpu.VMEM(*back)] * 2 + [pltpu.VMEM((len(LATE), 3 * short, 4 * LANES), bf16)],
    )[0].reshape(DEVICES, rows, LANES)
    field = lax.all_to_all(shares, everywhere, split_axis=0, concat_axis=0, tiled=True)
    return call(
        gate_kernel,
        "gate",
        [gate_rows, key_rows, value_rows, skip_bias.reshape(1, channels), field],
        [((rows, channels), bf16)],
    )[0]


def solution(mesh):
    placed = (
        P(("seq", "ch"), None),
        P(("seq", "ch"), None),
        P(("seq", "ch"), None),
        P(None, "seq", None, "ch"),
        P(),
    )
    shape = dict(mesh.shape)
    body = halves if (shape["seq"], shape["ch"]) == (SEQ, CH) else any_mesh
    return jax.shard_map(
        body, mesh=mesh, in_specs=placed, out_specs=P(("seq", "ch"), None), check_vma=False
    )
```

```python
import functools
import math

import jax
import jax.numpy as jnp
import numpy as np
from jax import lax
from jax.experimental import pallas as pl
from jax.experimental.pallas import tpu as pltpu
from jax.sharding import PartitionSpec as P

highest = lax.Precision.HIGHEST
LANES = 128
MIB = 1 << 20


def phase_table(first, second, modulus):
    turns = first[:, None] * second[None, :] % modulus
    angles = turns.astype(jnp.float32) * (2.0 * math.pi / modulus)
    return (jnp.cos(angles), jnp.sin(angles))


def convolve(product, spectrum):
    seq_count = lax.axis_size("seq")
    tokens, width = product.shape
    length_two = 2 * seq_count * tokens
    offsets = jnp.arange(2 * seq_count, dtype=jnp.int32)
    places = jnp.arange(seq_count, dtype=jnp.int32)
    residues = jnp.arange(tokens, dtype=jnp.int32)
    off_cos, off_sin = phase_table(offsets, places, 2 * seq_count)
    res_cos, res_sin = phase_table(residues, residues, tokens)
    block = tokens // seq_count
    device = lax.axis_index("seq")
    pieces = lax.all_to_all(
        product.reshape(1, tokens, width), "seq", split_axis=1, concat_axis=0, tiled=True
    )
    values = pieces.astype(jnp.float32)
    real_part = jnp.einsum("kp,prc->krc", off_cos, values, precision=highest)
    imag_part = -jnp.einsum("kp,prc->krc", off_sin, values, precision=highest)
    own_rows = device * block + jnp.arange(block, dtype=jnp.int32)
    tw_cos, tw_sin = phase_table(offsets, own_rows, length_two)
    tw_cos = tw_cos[:, :, None]
    tw_sin = tw_sin[:, :, None]
    real_part, imag_part = (
        real_part * tw_cos + imag_part * tw_sin,
        imag_part * tw_cos - real_part * tw_sin,
    )
    real_part, imag_part = (
        lax.all_to_all(real_part, "seq", split_axis=0, concat_axis=1, tiled=True),
        lax.all_to_all(imag_part, "seq", split_axis=0, concat_axis=1, tiled=True),
    )
    real_next = jnp.einsum("grc,rs->gsc", real_part, res_cos, precision=highest) + jnp.einsum(
        "grc,rs->gsc", imag_part, res_sin, precision=highest
    )
    imag_next = jnp.einsum("grc,rs->gsc", imag_part, res_cos, precision=highest) - jnp.einsum(
        "grc,rs->gsc", real_part, res_sin, precision=highest
    )
    spec_real = spectrum[0]
    spec_imag = spectrum[1]
    real_part = real_next * spec_real - imag_next * spec_imag
    imag_part = real_next * spec_imag + imag_next * spec_real
    real_next = jnp.einsum("gsc,sr->grc", real_part, res_cos, precision=highest) - jnp.einsum(
        "gsc,sr->grc", imag_part, res_sin, precision=highest
    )
    imag_next = jnp.einsum("gsc,sr->grc", imag_part, res_cos, precision=highest) + jnp.einsum(
        "gsc,sr->grc", real_part, res_sin, precision=highest
    )
    own_offsets = 2 * device + jnp.arange(2, dtype=jnp.int32)
    un_cos, un_sin = phase_table(own_offsets, residues, length_two)
    un_cos = un_cos[:, :, None]
    un_sin = un_sin[:, :, None]
    real_part = real_next * un_cos - imag_next * un_sin
    imag_part = imag_next * un_cos + real_next * un_sin
    real_part, imag_part = (
        lax.all_to_all(real_part, "seq", split_axis=1, concat_axis=0, tiled=True),
        lax.all_to_all(imag_part, "seq", split_axis=1, concat_axis=0, tiled=True),
    )
    field = jnp.einsum("kp,krc->prc", off_cos, real_part, precision=highest) - jnp.einsum(
        "kp,krc->prc", off_sin, imag_part, precision=highest
    )
    field = field / length_two
    field = lax.all_to_all(field, "seq", split_axis=0, concat_axis=1, tiled=True)
    return field.reshape(tokens, width)


def any_mesh(gate_rows, key_rows, value_rows, spectrum, skip_bias):
    own = (key_rows.astype(jnp.float32) * value_rows.astype(jnp.float32)).astype(jnp.bfloat16)
    product = lax.all_to_all(own, "ch", split_axis=1, concat_axis=0, tiled=True)
    field = convolve(product, spectrum)
    field = lax.all_to_all(field, "ch", split_axis=0, concat_axis=1, tiled=True)
    gated = gate_rows.astype(jnp.float32) * (
        field + skip_bias[None, :] * own.astype(jnp.float32)
    )
    return gated.astype(jnp.bfloat16)


SEQ, CH, HALF = 8, 4, 4
DEVICES = SEQ * CH
ROOT = math.sqrt(0.5)
EARLY, LATE = (0, 1, 3), (2,)
VMEM = pl.BlockSpec(memory_space=pltpu.VMEM)
STEP = 16


def swap(array, axis, mask, count):
    return lax.ppermute(array, axis, [(i, i ^ mask) for i in range(count)])


def columns_of(device):
    seq, ch = divmod(device, CH)
    return pl.ds((ch * HALF + seq % HALF) * LANES, LANES)


def rows_at(index, first=0):
    return pl.ds(pl.multiple_of(first + index * STEP, STEP), STEP)


def times(a, b):
    return a[0] * b[0] - a[1] * b[1], a[0] * b[1] + a[1] * b[0]


def root_16(power):
    return math.cos(power * math.pi / 8), math.sin(power * math.pi / 8)


def product_kernel(key_hbm, value_hbm, out_ref, key, value, sems):
    groups = DEVICES // 2
    width = key.shape[1] // CH
    copies = []
    for ch in range(CH):
        at = pl.ds(ch * width, width)
        copies.append(
            [
                pltpu.make_async_copy(source.at[:, at], to.at[:, at], sems.at[which, ch])
                for which, (source, to) in enumerate(((key_hbm, key), (value_hbm, value)))
            ]
        )
        for copy in copies[-1]:
            copy.start()
    for ch in range(CH):
        for copy in copies[ch]:
            copy.wait()
        for member in range(HALF):
            device = member * CH + ch
            at = columns_of(device)
            product = (key[:, at].astype(jnp.float32) * value[:, at].astype(jnp.float32)).astype(jnp.bfloat16)
            out_ref[device] = product
            out_ref[device + groups] = product


def spectrum_kernel(place_ref, *refs):
    count = len(refs) // 2
    spec, members = refs[:count], refs[count:]
    rows = members[0].shape[3]
    for member in range(count):
        for part in range(2):
            for odd in range(2):
                for bit in range(2):
                    values = spec[member][part, odd, pl.ds(bit, rows, stride=2), :]
                    members[member][part, odd, bit] = values.astype(jnp.bfloat16)


def members_of(spectrum, which, steps=4):
    size = spectrum.shape[2]
    piece = size // steps
    place = (lax.axis_index("seq") % HALF).astype(jnp.int32).reshape(1)
    spec_blocks = [
        pl.BlockSpec((2, 2, piece, LANES), lambda i, place, member=member: (0, 0, i, place[0] ^ member))
        for member in which
    ]
    return pl.pallas_call(
        spectrum_kernel,
        grid_spec=pltpu.PrefetchScalarGridSpec(
            num_scalar_prefetch=1,
            grid=(steps,),
            in_specs=spec_blocks,
            out_specs=[pl.BlockSpec((2, 2, 2, piece // 2, LANES), lambda i, place: (0, 0, 0, i, 0))] * len(which),
        ),
        out_shape=[jax.ShapeDtypeStruct((2, 2, 2, size // 2, LANES), jnp.bfloat16)] * len(which),
        compiler_params=pltpu.CompilerParams(vmem_limit_bytes=56 * MIB),
        name="spectrum",
    )(place, *[spectrum] * len(which))


def four_real(a0, a1, a2, a3):
    even, odd = a0 + a2, a1 + a3
    less, more = (a1 - a3) * ROOT, odd * ROOT
    return (
        (even + odd, None),
        (a0 + less, -(a2 + more)),
        (a0 - a2, a3 - a1),
        (a0 - less, a2 - more),
        (even - odd, None),
    )


def residues_of(values, sign):
    even = four_real(*values[0::2])
    odd = four_real(*[v * sign for v in values[1::2]])
    out = [None] * SEQ
    out[0] = (even[0][0] + odd[0][0], None)
    out[4] = (even[4][0], -odd[4][0])
    for j in (1, 2, 3):
        turned = times(odd[j], root_16(-j))
        out[j] = (even[j][0] + turned[0], even[j][1] + turned[1])
        out[8 - j] = (even[j][0] - turned[0], turned[1] - even[j][1])
    return out


def four_back(zero, four, one, two, three):
    plus, minus = zero + four, zero - four
    half_way = (one[0] - three[0]) * ROOT
    across = (one[1] + three[1]) * ROOT
    return (
        plus + two[0] + (one[0] + three[0]),
        minus - two[1] + (half_way - across),
        plus - two[0] + (three[1] - one[1]),
        minus + two[1] - (half_way + across),
    )


def blocks_of(parts):
    sums, turned = [], []
    for j in (1, 2, 3):
        a, b = parts[j], parts[8 - j]
        sums.append((a[0] + b[0], a[1] - b[1]))
        turned.append(times((a[0] - b[0], a[1] + b[1]), root_16(j)))
    even = four_back(parts[0][0], parts[4][0], *sums)
    odd = four_back(parts[0][0], -parts[4][1], *turned)
    return [value for pair in zip(even, odd) for value in pair]


def sign_of_half():
    return jnp.where(lax.axis_index("seq") < HALF, 1.0, -1.0).astype(jnp.float32)


def turn_table(size):
    angles = np.arange(2 * SEQ)[:, None] * np.arange(size)[None, :] * (2.0 * np.pi / (2 * SEQ * size))
    angles = angles.reshape(2, SEQ, size)
    between = np.broadcast_to(np.arange(size) * (2.0 * np.pi / size), (2, 1, size))
    angles = np.concatenate([angles, between], axis=1)
    table = np.stack([np.cos(angles), np.sin(angles)], axis=2).astype(np.float32)
    return jnp.asarray(np.repeat(table[..., None], LANES, axis=-1))


def forward_kernel(tokens, table, dft_ref, re_ref, im_ref, stage):
    sign = sign_of_half()
    size = tokens.shape[1]
    short = size // 2

    def rows_of(index, carry):
        both = []
        for first in (0, short):
            at = rows_at(index, first)
            parts = residues_of([tokens[p, at, :].astype(jnp.float32) for p in range(SEQ)], sign)
            turned = []
            for j, (real, imag) in enumerate(parts):
                cos, sin = table[j, 0, at, :], table[j, 1, at, :]
                if imag is None:
                    turned.append((real * cos, -(real * sin)))
                else:
                    turned.append((real * cos + imag * sin, imag * cos - real * sin))
            both.append(turned)
        at = rows_at(index)
        cos, sin = table[SEQ, 0, at, :], table[SEQ, 1, at, :]
        for j in range(SEQ):
            a, b = both[0][j], both[1][j]
            less = a[0] - b[0], a[1] - b[1]
            pair = (a[0] + b[0], a[1] + b[1]), (less[0] * cos + less[1] * sin, less[1] * cos - less[0] * sin)
            for bit, (real, imag) in enumerate(pair):
                to = pl.ds((bit * SEQ + j) * LANES, LANES)
                real = real.astype(jnp.bfloat16)
                stage[at, to] = real
                stage[rows_at(index, short), to] = imag.astype(jnp.bfloat16)
                stage[rows_at(index, size), to] = -real
        return carry

    lax.fori_loop(0, short // STEP, rows_of, 0)
    re_ref[...] = jnp.dot(dft_ref[...], stage[pl.ds(0, size), :], preferred_element_type=jnp.float32)
    im_ref[...] = jnp.dot(dft_ref[...], stage[pl.ds(short, size), :], preferred_element_type=jnp.float32)


def filter_members(members, spec, re_ref, im_ref, dft_ref, back_re, back_im, stage):
    place = lax.axis_index("seq") % HALF
    short = re_ref.shape[0]
    size = 2 * short
    for index, member in enumerate(members):
        for odd in range(2):
            for bit in range(2):
                column = bit * SEQ + 2 * (place ^ member) + odd
                at = pl.ds(pl.multiple_of(column * LANES, LANES), LANES)
                h = spec[index][0, odd, bit].astype(jnp.float32), spec[index][1, odd, bit].astype(jnp.float32)
                y_re, y_im = times((re_ref[:, at], im_ref[:, at]), h)
                y_re, y_im = y_re.astype(jnp.bfloat16), y_im.astype(jnp.bfloat16)
                to = pl.ds((odd * 2 + bit) * LANES, LANES)
                stage[index, pl.ds(0, short), to] = y_im
                stage[index, pl.ds(short, short), to] = y_re
                stage[index, pl.ds(size, short), to] = -y_im
        back_im[place ^ member] = jnp.dot(
            dft_ref[...], stage[index, pl.ds(0, size), :], preferred_element_type=jnp.float32
        )
        back_re[place ^ member] = jnp.dot(
            dft_ref[...], stage[index, pl.ds(short, size), :], preferred_element_type=jnp.float32
        )


def early_kernel(*refs):
    spec, (re_ref, im_ref, dft_ref, back_re, back_im, stage) = refs[: len(EARLY)], refs[len(EARLY) :]
    filter_members(EARLY, spec, re_ref, im_ref, dft_ref, back_re, back_im, stage)


def late_kernel(*refs):
    spec, refs = refs[: len(LATE)], refs[len(LATE) :]
    early_re, early_im, re_ref, im_ref, table, dft_ref, out_ref, back_re, back_im, stage = refs
    sign = sign_of_half()
    place = lax.axis_index("seq") % HALF
    short = re_ref.shape[0]
    size = 2 * short
    filter_members(LATE, spec, re_ref, im_ref, dft_ref, back_re, back_im, stage)
    for member in EARLY:
        back_re[place ^ member] = early_re[place ^ member]
        back_im[place ^ member] = early_im[place ^ member]
    scale = 1.0 / (2 * SEQ * size)

    def rows_of(index, carry):
        at = rows_at(index)
        late = rows_at(index, short)
        cos, sin = table[SEQ, 0, at, :], table[SEQ, 1, at, :]
        parts = [], []
        for j in range(SEQ):
            pair = []
            for bit in range(2):
                to = pl.ds((j % 2 * 2 + bit) * LANES, LANES)
                pair.append((back_re[j // 2, at, to], back_im[j // 2, at, to]))
            a, b = pair[0], times(pair[1], (cos, sin))
            parts[0].append(times((a[0] + b[0], a[1] + b[1]), (table[j, 0, at, :], table[j, 1, at, :])))
            parts[1].append(times((a[0] - b[0], a[1] - b[1]), (table[j, 0, late, :], table[j, 1, late, :])))
        for where, values in zip((at, late), parts):
            for p, value in enumerate(blocks_of(values)):
                out_ref[p, where, :] = (value * (scale * sign if p % 2 else scale)).astype(jnp.bfloat16)
        return carry

    lax.fori_loop(0, short // STEP, rows_of, 0)


def table_kernel(after, table_hbm, table, sem):
    copy = pltpu.make_async_copy(table_hbm.at[lax.axis_index("seq") // HALF], table, sem)
    copy.start()
    copy.wait()


def gate_kernel(gate_ref, key_ref, value_ref, skip_ref, field_ref, out_ref):
    for device in range(DEVICES // 2):
        at = columns_of(device)
        product = (key_ref[:, at].astype(jnp.float32) * value_ref[:, at].astype(jnp.float32)).astype(jnp.bfloat16)
        field = field_ref[device].astype(jnp.float32) + field_ref[device + DEVICES // 2].astype(jnp.float32)
        gated = gate_ref[:, at].astype(jnp.float32) * (field + skip_ref[:, at] * product.astype(jnp.float32))
        out_ref[:, at] = gated.astype(jnp.bfloat16)


def call(kernel, name, ins, outs, scratch=(), limit=24 * MIB, hbm=(), cost=None):
    return pl.pallas_call(
        kernel,
        out_shape=tuple(jax.ShapeDtypeStruct(shape, dtype) for shape, dtype in outs),
        in_specs=[pl.BlockSpec(memory_space=pl.ANY) if index in hbm else VMEM for index, _ in enumerate(ins)],
        out_specs=tuple(VMEM for _ in outs),
        scratch_shapes=list(scratch),
        compiler_params=pltpu.CompilerParams(vmem_limit_bytes=limit),
        cost_estimate=cost,
        name=name,
    )(*ins)


def halves(gate_rows, key_rows, value_rows, spectrum, skip_bias):
    bf16, f32 = jnp.bfloat16, jnp.float32
    rows, channels = key_rows.shape
    size = rows * CH
    short = size // 2
    everywhere = ("seq", "ch")

    angles = np.arange(short)[:, None] * np.arange(short)[None, :] % short * (2.0 * np.pi / short)
    dft = jnp.asarray(np.concatenate([np.cos(angles), np.sin(angles)], axis=1), bf16)
    table = turn_table(size)

    sends = call(
        product_kernel,
        "product",
        [key_rows, value_rows],
        [((DEVICES, rows, LANES), bf16)],
        [pltpu.VMEM((rows, channels), bf16)] * 2 + [pltpu.SemaphoreType.DMA((2, CH))],
        limit=56 * MIB,
        hbm=(0, 1),
    )[0]
    (last,) = members_of(spectrum, (3,), steps=2)
    last = swap(last, "seq", 3, SEQ)
    cost = pl.CostEstimate(flops=40000000000, bytes_accessed=1 << 20, transcendentals=0)
    (table,) = call(
        table_kernel,
        "table",
        [last, table],
        [(table.shape[1:], f32)],
        [pltpu.SemaphoreType.DMA],
        hbm=(0, 1),
        cost=cost,
    )
    spec = members_of(spectrum, (0, 1, 2))
    tokens = lax.all_to_all(sends, everywhere, split_axis=0, concat_axis=0, tiled=True).reshape(SEQ, size, LANES)
    spec = [spec[0]] + [swap(spec[member], "seq", member, SEQ) for member in (1, 2)] + [last]
    freq = call(
        forward_kernel,
        "forward",
        [tokens, table, dft],
        [((short, 2 * SEQ * LANES), f32)] * 2,
        [pltpu.VMEM((3 * short, 2 * SEQ * LANES), bf16)],
    )
    back = ((HALF, short, 4 * LANES), f32)
    early = call(
        early_kernel,
        "early_members",
        [*[spec[member] for member in EARLY], *freq, dft],
        [back] * 2,
        [pltpu.VMEM((len(EARLY), 3 * short, 4 * LANES), bf16)],
    )
    shares = call(
        late_kernel,
        "late_member",
        [*[spec[member] for member in LATE], *early, *freq, table, dft],
        [((SEQ, size, LANES), bf16)],
        [pltpu.VMEM(*back)] * 2 + [pltpu.VMEM((len(LATE), 3 * short, 4 * LANES), bf16)],
    )[0].reshape(DEVICES, rows, LANES)
    field = lax.all_to_all(shares, everywhere, split_axis=0, concat_axis=0, tiled=True)
    return call(
        gate_kernel,
        "gate",
        [gate_rows, key_rows, value_rows, skip_bias.reshape(1, channels), field],
        [((rows, channels), bf16)],
    )[0]


def solution(mesh):
    placed = (
        P(("seq", "ch"), None),
        P(("seq", "ch"), None),
        P(("seq", "ch"), None),
        P(None, "seq", None, "ch"),
        P(),
    )
    shape = dict(mesh.shape)
    body = halves if (shape["seq"], shape["ch"]) == (SEQ, CH) else any_mesh
    return jax.shard_map(
        body, mesh=mesh, in_specs=placed, out_specs=P(("seq", "ch"), None), check_vma=False
    )
```

```python
import functools
import math

import jax
import jax.numpy as jnp
import numpy as np
from jax import lax
from jax.experimental import pallas as pl
from jax.experimental.pallas import tpu as pltpu
from jax.sharding import PartitionSpec as P

highest = lax.Precision.HIGHEST
LANES = 128
MIB = 1 << 20


def phase_table(first, second, modulus):
    turns = first[:, None] * second[None, :] % modulus
    angles = turns.astype(jnp.float32) * (2.0 * math.pi / modulus)
    return (jnp.cos(angles), jnp.sin(angles))


def convolve(product, spectrum):
    seq_count = lax.axis_size("seq")
    tokens, width = product.shape
    length_two = 2 * seq_count * tokens
    offsets = jnp.arange(2 * seq_count, dtype=jnp.int32)
    places = jnp.arange(seq_count, dtype=jnp.int32)
    residues = jnp.arange(tokens, dtype=jnp.int32)
    off_cos, off_sin = phase_table(offsets, places, 2 * seq_count)
    res_cos, res_sin = phase_table(residues, residues, tokens)
    block = tokens // seq_count
    device = lax.axis_index("seq")
    pieces = lax.all_to_all(
        product.reshape(1, tokens, width), "seq", split_axis=1, concat_axis=0, tiled=True
    )
    values = pieces.astype(jnp.float32)
    real_part = jnp.einsum("kp,prc->krc", off_cos, values, precision=highest)
    imag_part = -jnp.einsum("kp,prc->krc", off_sin, values, precision=highest)
    own_rows = device * block + jnp.arange(block, dtype=jnp.int32)
    tw_cos, tw_sin = phase_table(offsets, own_rows, length_two)
    tw_cos = tw_cos[:, :, None]
    tw_sin = tw_sin[:, :, None]
    real_part, imag_part = (
        real_part * tw_cos + imag_part * tw_sin,
        imag_part * tw_cos - real_part * tw_sin,
    )
    real_part, imag_part = (
        lax.all_to_all(real_part, "seq", split_axis=0, concat_axis=1, tiled=True),
        lax.all_to_all(imag_part, "seq", split_axis=0, concat_axis=1, tiled=True),
    )
    real_next = jnp.einsum("grc,rs->gsc", real_part, res_cos, precision=highest) + jnp.einsum(
        "grc,rs->gsc", imag_part, res_sin, precision=highest
    )
    imag_next = jnp.einsum("grc,rs->gsc", imag_part, res_cos, precision=highest) - jnp.einsum(
        "grc,rs->gsc", real_part, res_sin, precision=highest
    )
    spec_real = spectrum[0]
    spec_imag = spectrum[1]
    real_part = real_next * spec_real - imag_next * spec_imag
    imag_part = real_next * spec_imag + imag_next * spec_real
    real_next = jnp.einsum("gsc,sr->grc", real_part, res_cos, precision=highest) - jnp.einsum(
        "gsc,sr->grc", imag_part, res_sin, precision=highest
    )
    imag_next = jnp.einsum("gsc,sr->grc", imag_part, res_cos, precision=highest) + jnp.einsum(
        "gsc,sr->grc", real_part, res_sin, precision=highest
    )
    own_offsets = 2 * device + jnp.arange(2, dtype=jnp.int32)
    un_cos, un_sin = phase_table(own_offsets, residues, length_two)
    un_cos = un_cos[:, :, None]
    un_sin = un_sin[:, :, None]
    real_part = real_next * un_cos - imag_next * un_sin
    imag_part = imag_next * un_cos + real_next * un_sin
    real_part, imag_part = (
        lax.all_to_all(real_part, "seq", split_axis=1, concat_axis=0, tiled=True),
        lax.all_to_all(imag_part, "seq", split_axis=1, concat_axis=0, tiled=True),
    )
    field = jnp.einsum("kp,krc->prc", off_cos, real_part, precision=highest) - jnp.einsum(
        "kp,krc->prc", off_sin, imag_part, precision=highest
    )
    field = field / length_two
    field = lax.all_to_all(field, "seq", split_axis=0, concat_axis=1, tiled=True)
    return field.reshape(tokens, width)


def any_mesh(gate_rows, key_rows, value_rows, spectrum, skip_bias):
    own = (key_rows.astype(jnp.float32) * value_rows.astype(jnp.float32)).astype(jnp.bfloat16)
    product = lax.all_to_all(own, "ch", split_axis=1, concat_axis=0, tiled=True)
    field = convolve(product, spectrum)
    field = lax.all_to_all(field, "ch", split_axis=0, concat_axis=1, tiled=True)
    gated = gate_rows.astype(jnp.float32) * (
        field + skip_bias[None, :] * own.astype(jnp.float32)
    )
    return gated.astype(jnp.bfloat16)


SEQ, CH, HALF = 8, 4, 4
DEVICES = SEQ * CH
ROOT = math.sqrt(0.5)
EARLY, LATE = (0, 1, 3), (2,)
NEAR = 64
VMEM = pl.BlockSpec(memory_space=pltpu.VMEM)
SMEM = pl.BlockSpec(memory_space=pltpu.SMEM)
STEP = 16


def swap(array, axis, mask, count):
    return lax.ppermute(array, axis, [(i, i ^ mask) for i in range(count)])


def columns_of(device):
    seq, ch = divmod(device, CH)
    return pl.ds((ch * HALF + seq % HALF) * LANES, LANES)


def rows_at(index, first=0):
    return pl.ds(pl.multiple_of(first + index * STEP, STEP), STEP)


def times(a, b):
    return a[0] * b[0] - a[1] * b[1], a[0] * b[1] + a[1] * b[0]


def root_16(power):
    return math.cos(power * math.pi / 8), math.sin(power * math.pi / 8)


def product_kernel(key_hbm, value_hbm, out_ref, key, value, sems):
    groups = DEVICES // 2
    width = key.shape[1] // CH
    copies = []
    for ch in range(CH):
        at = pl.ds(ch * width, width)
        copies.append(
            [
                pltpu.make_async_copy(source.at[:, at], to.at[:, at], sems.at[which, ch])
                for which, (source, to) in enumerate(((key_hbm, key), (value_hbm, value)))
            ]
        )
        for copy in copies[-1]:
            copy.start()
    for ch in range(CH):
        for copy in copies[ch]:
            copy.wait()
        for member in range(HALF):
            device = member * CH + ch
            at = columns_of(device)
            product = (key[:, at].astype(jnp.float32) * value[:, at].astype(jnp.float32)).astype(jnp.bfloat16)
            out_ref[device] = product
            out_ref[device + groups] = product


def spectrum_kernel(place_ref, *refs):
    count = len(refs) // 2
    spec, members = refs[:count], refs[count:]
    rows = members[0].shape[3]
    for member in range(count):
        for part in range(2):
            for odd in range(2):
                for bit in range(2):
                    values = spec[member][part, odd, pl.ds(bit, rows, stride=2), :]
                    members[member][part, odd, bit] = values.astype(jnp.bfloat16)


def members_of(spectrum, which, steps=4):
    size = spectrum.shape[2]
    piece = size // steps
    place = (lax.axis_index("seq") % HALF).astype(jnp.int32).reshape(1)
    spec_blocks = [
        pl.BlockSpec((2, 2, piece, LANES), lambda i, place, member=member: (0, 0, i, place[0] ^ member))
        for member in which
    ]
    return pl.pallas_call(
        spectrum_kernel,
        grid_spec=pltpu.PrefetchScalarGridSpec(
            num_scalar_prefetch=1,
            grid=(steps,),
            in_specs=spec_blocks,
            out_specs=[pl.BlockSpec((2, 2, 2, piece // 2, LANES), lambda i, place: (0, 0, 0, i, 0))] * len(which),
        ),
        out_shape=[jax.ShapeDtypeStruct((2, 2, 2, size // 2, LANES), jnp.bfloat16)] * len(which),
        compiler_params=pltpu.CompilerParams(vmem_limit_bytes=56 * MIB),
        name="spectrum",
    )(place, *[spectrum] * len(which))


def four_real(a0, a1, a2, a3):
    even, odd = a0 + a2, a1 + a3
    less, more = (a1 - a3) * ROOT, odd * ROOT
    return (
        (even + odd, None),
        (a0 + less, -(a2 + more)),
        (a0 - a2, a3 - a1),
        (a0 - less, a2 - more),
        (even - odd, None),
    )


def residues_of(values, sign):
    even = four_real(*values[0::2])
    odd = four_real(*[v * sign for v in values[1::2]])
    out = [None] * SEQ
    out[0] = (even[0][0] + odd[0][0], None)
    out[4] = (even[4][0], -odd[4][0])
    for j in (1, 2, 3):
        turned = times(odd[j], root_16(-j))
        out[j] = (even[j][0] + turned[0], even[j][1] + turned[1])
        out[8 - j] = (even[j][0] - turned[0], turned[1] - even[j][1])
    return out


def four_back(zero, four, one, two, three):
    plus, minus = zero + four, zero - four
    half_way = (one[0] - three[0]) * ROOT
    across = (one[1] + three[1]) * ROOT
    return (
        plus + two[0] + (one[0] + three[0]),
        minus - two[1] + (half_way - across),
        plus - two[0] + (three[1] - one[1]),
        minus + two[1] - (half_way + across),
    )


def blocks_of(parts):
    sums, turned = [], []
    for j in (1, 2, 3):
        a, b = parts[j], parts[8 - j]
        sums.append((a[0] + b[0], a[1] - b[1]))
        turned.append(times((a[0] - b[0], a[1] + b[1]), root_16(j)))
    even = four_back(parts[0][0], parts[4][0], *sums)
    odd = four_back(parts[0][0], -parts[4][1], *turned)
    return [value for pair in zip(even, odd) for value in pair]


def sign_of_half():
    return jnp.where(lax.axis_index("seq") < HALF, 1.0, -1.0).astype(jnp.float32)


def turn_table(size):
    angles = np.arange(2 * SEQ)[:, None] * np.arange(size)[None, :] * (2.0 * np.pi / (2 * SEQ * size))
    angles = angles.reshape(2, SEQ, size)
    between = np.broadcast_to(np.arange(size) * (2.0 * np.pi / size), (2, 1, size))
    angles = np.concatenate([angles, between], axis=1)
    table = np.stack([np.cos(angles), np.sin(angles)], axis=2).astype(np.float32)
    return jnp.asarray(np.repeat(table[..., None], LANES, axis=-1))


def split_table(size):
    turns = np.arange(2 * SEQ).reshape(2, SEQ) / (2 * SEQ * size)
    turns = 2 * np.pi * np.concatenate([turns, np.full((2, 1), 1 / size)], axis=1)
    near, far = (turns[:, :, None] * tokens for tokens in (np.arange(NEAR), np.arange(0, size, NEAR)))
    near = np.repeat(np.stack([np.cos(near), np.sin(near)], axis=2)[..., None], LANES, axis=-1)
    far = np.stack([np.cos(far), np.sin(far)], axis=3).reshape(-1)
    return jnp.asarray(near, jnp.float32), jnp.asarray(far, jnp.float32)


def forward_kernel(tokens, near, far, dft_ref, re_ref, im_ref, stage):
    half = lax.axis_index("seq") // HALF
    sign = sign_of_half()
    size = tokens.shape[1]
    short = size // 2
    chunks = NEAR // STEP

    def twiddle(j, a, at):
        index = ((half * (SEQ + 1) + j) * (size // NEAR) + a) * 2
        return times((near[j, 0, at, :], near[j, 1, at, :]), (far[index], far[index + 1]))

    def rows_of(index, carry):
        a = index // chunks
        near_at = rows_at(index % chunks)
        both = []
        for late in range(2):
            at = rows_at(index, late * short)
            parts = residues_of([tokens[p, at, :].astype(jnp.float32) for p in range(SEQ)], sign)
            turned = []
            for j, (real, imag) in enumerate(parts):
                cos, sin = twiddle(j, a + late * (short // NEAR), near_at)
                if imag is None:
                    turned.append((real * cos, -(real * sin)))
                else:
                    turned.append((real * cos + imag * sin, imag * cos - real * sin))
            both.append(turned)
        at = rows_at(index)
        cos, sin = twiddle(SEQ, a, near_at)
        for j in range(SEQ):
            x, y = both[0][j], both[1][j]
            less = x[0] - y[0], x[1] - y[1]
            pair = (x[0] + y[0], x[1] + y[1]), (less[0] * cos + less[1] * sin, less[1] * cos - less[0] * sin)
            for bit, (real, imag) in enumerate(pair):
                to = pl.ds((bit * SEQ + j) * LANES, LANES)
                real = real.astype(jnp.bfloat16)
                stage[at, to] = real
                stage[rows_at(index, short), to] = imag.astype(jnp.bfloat16)
                stage[rows_at(index, size), to] = -real
        return carry

    lax.fori_loop(0, short // STEP, rows_of, 0, unroll=2)
    re_ref[...] = jnp.dot(dft_ref[...], stage[pl.ds(0, size), :], preferred_element_type=jnp.float32)
    im_ref[...] = jnp.dot(dft_ref[...], stage[pl.ds(short, size), :], preferred_element_type=jnp.float32)


def filter_members(members, spec, re_ref, im_ref, dft_ref, back_re, back_im, stage):
    place = lax.axis_index("seq") % HALF
    short = re_ref.shape[0]
    size = 2 * short
    for index, member in enumerate(members):
        for odd in range(2):
            for bit in range(2):
                column = bit * SEQ + 2 * (place ^ member) + odd
                at = pl.ds(pl.multiple_of(column * LANES, LANES), LANES)
                h = spec[index][0, odd, bit].astype(jnp.float32), spec[index][1, odd, bit].astype(jnp.float32)
                y_re, y_im = times((re_ref[:, at], im_ref[:, at]), h)
                y_re, y_im = y_re.astype(jnp.bfloat16), y_im.astype(jnp.bfloat16)
                to = pl.ds((odd * 2 + bit) * LANES, LANES)
                stage[index, pl.ds(0, short), to] = y_im
                stage[index, pl.ds(short, short), to] = y_re
                stage[index, pl.ds(size, short), to] = -y_im
        back_im[place ^ member] = jnp.dot(
            dft_ref[...], stage[index, pl.ds(0, size), :], preferred_element_type=jnp.float32
        )
        back_re[place ^ member] = jnp.dot(
            dft_ref[...], stage[index, pl.ds(short, size), :], preferred_element_type=jnp.float32
        )


def early_kernel(*refs):
    spec, (re_ref, im_ref, dft_ref, back_re, back_im, stage) = refs[: len(EARLY)], refs[len(EARLY) :]
    filter_members(EARLY, spec, re_ref, im_ref, dft_ref, back_re, back_im, stage)


def late_kernel(*refs):
    spec, refs = refs[: len(LATE)], refs[len(LATE) :]
    early_re, early_im, re_ref, im_ref, table, dft_ref, out_ref, back_re, back_im, stage = refs
    sign = sign_of_half()
    place = lax.axis_index("seq") % HALF
    short = re_ref.shape[0]
    size = 2 * short
    filter_members(LATE, spec, re_ref, im_ref, dft_ref, back_re, back_im, stage)
    for member in EARLY:
        back_re[place ^ member] = early_re[place ^ member]
        back_im[place ^ member] = early_im[place ^ member]
    scale = 1.0 / (2 * SEQ * size)

    def rows_of(index, carry):
        at = rows_at(index)
        late = rows_at(index, short)
        cos, sin = table[SEQ, 0, at, :], table[SEQ, 1, at, :]
        parts = [], []
        for j in range(SEQ):
            pair = []
            for bit in range(2):
                to = pl.ds((j % 2 * 2 + bit) * LANES, LANES)
                pair.append((back_re[j // 2, at, to], back_im[j // 2, at, to]))
            a, b = pair[0], times(pair[1], (cos, sin))
            parts[0].append(times((a[0] + b[0], a[1] + b[1]), (table[j, 0, at, :], table[j, 1, at, :])))
            parts[1].append(times((a[0] - b[0], a[1] - b[1]), (table[j, 0, late, :], table[j, 1, late, :])))
        for where, values in zip((at, late), parts):
            for p, value in enumerate(blocks_of(values)):
                out_ref[p, where, :] = (value * (scale * sign if p % 2 else scale)).astype(jnp.bfloat16)
        return carry

    lax.fori_loop(0, short // STEP, rows_of, 0, unroll=2)


def table_kernel(after, table_hbm, near_hbm, table, near, sems):
    half = lax.axis_index("seq") // HALF
    copies = [
        pltpu.make_async_copy(source.at[half], to, sems.at[index])
        for index, (source, to) in enumerate(((table_hbm, table), (near_hbm, near)))
    ]
    for copy in copies:
        copy.start()
    for copy in copies:
        copy.wait()


def gate_kernel(gate_ref, key_ref, value_ref, skip_ref, field_ref, out_hbm, held, sems):
    copies = []
    for ch in range(CH):
        for member in range(HALF):
            device = member * CH + ch
            at = columns_of(device)
            product = (key_ref[:, at].astype(jnp.float32) * value_ref[:, at].astype(jnp.float32)).astype(jnp.bfloat16)
            field = field_ref[device].astype(jnp.float32) + field_ref[device + DEVICES // 2].astype(jnp.float32)
            gated = gate_ref[:, at].astype(jnp.float32) * (field + skip_ref[:, at] * product.astype(jnp.float32))
            held[:, at] = gated.astype(jnp.bfloat16)
        columns = pl.ds(ch * HALF * LANES, HALF * LANES)
        copies.append(pltpu.make_async_copy(held.at[:, columns], out_hbm.at[:, columns], sems.at[ch]))
        copies[-1].start()
    for copy in copies:
        copy.wait()


def call(kernel, name, ins, outs, scratch=(), limit=24 * MIB, hbm=(), cost=None, aliases=None, to_hbm=False):
    return pl.pallas_call(
        kernel,
        out_shape=tuple(jax.ShapeDtypeStruct(shape, dtype) for shape, dtype in outs),
        in_specs=[pl.BlockSpec(memory_space=pl.ANY) if index in hbm else SMEM if x.ndim == 1 else VMEM for index, x in enumerate(ins)],
        out_specs=tuple(pl.BlockSpec(memory_space=pl.ANY) if to_hbm else VMEM for _ in outs),
        scratch_shapes=list(scratch),
        compiler_params=pltpu.CompilerParams(vmem_limit_bytes=limit),
        cost_estimate=cost,
        input_output_aliases=aliases or {},
        name=name,
    )(*ins)


def halves(gate_rows, key_rows, value_rows, spectrum, skip_bias):
    bf16, f32 = jnp.bfloat16, jnp.float32
    rows, channels = key_rows.shape
    size = rows * CH
    short = size // 2
    everywhere = ("seq", "ch")

    angles = np.arange(short)[:, None] * np.arange(short)[None, :] % short * (2.0 * np.pi / short)
    dft = jnp.asarray(np.concatenate([np.cos(angles), np.sin(angles)], axis=1), bf16)
    table = turn_table(size)
    near, far = split_table(size)

    sends = call(
        product_kernel,
        "product",
        [key_rows, value_rows],
        [((DEVICES, rows, LANES), bf16)],
        [pltpu.VMEM((rows, channels), bf16)] * 2 + [pltpu.SemaphoreType.DMA((2, CH))],
        limit=56 * MIB,
        hbm=(0, 1),
    )[0]
    (last,) = members_of(spectrum, (3,), steps=2)
    last = swap(last, "seq", 3, SEQ)
    cost = pl.CostEstimate(flops=40000000000, bytes_accessed=1 << 20, transcendentals=0)
    table, near = call(
        table_kernel,
        "table",
        [last, table, near],
        [(table.shape[1:], f32), (near.shape[1:], f32)],
        [pltpu.SemaphoreType.DMA((2,))],
        hbm=(0, 1, 2),
        cost=cost,
    )
    spec = members_of(spectrum, (0, 1, 2))
    tokens = lax.all_to_all(sends, everywhere, split_axis=0, concat_axis=0, tiled=True).reshape(SEQ, size, LANES)
    spec = [spec[0]] + [swap(spec[member], "seq", member, SEQ) for member in (1, 2)] + [last]
    freq = call(
        forward_kernel,
        "forward",
        [tokens, near, far, dft],
        [((short, 2 * SEQ * LANES), f32)] * 2,
        [pltpu.VMEM((3 * short, 2 * SEQ * LANES), bf16)],
    )
    back = ((HALF, short, 4 * LANES), f32)
    early = call(
        early_kernel,
        "early_members",
        [*[spec[member] for member in EARLY], *freq, dft],
        [back] * 2,
        [pltpu.VMEM((len(EARLY), 3 * short, 4 * LANES), bf16)],
    )
    shares = call(
        late_kernel,
        "late_member",
        [*[spec[member] for member in LATE], *early, *freq, table, dft],
        [((SEQ, size, LANES), bf16)],
        [pltpu.VMEM(*back)] * 2 + [pltpu.VMEM((len(LATE), 3 * short, 4 * LANES), bf16)],
    )[0].reshape(DEVICES, rows, LANES)
    field = lax.all_to_all(shares, everywhere, split_axis=0, concat_axis=0, tiled=True)
    return call(
        gate_kernel,
        "gate",
        [gate_rows, key_rows, value_rows, skip_bias.reshape(1, channels), field],
        [((rows, channels), bf16)],
        [pltpu.VMEM((rows, channels), bf16), pltpu.SemaphoreType.DMA((CH,))],
        to_hbm=True,
    )[0]


def solution(mesh):
    placed = (
        P(("seq", "ch"), None),
        P(("seq", "ch"), None),
        P(("seq", "ch"), None),
        P(None, "seq", None, "ch"),
        P(),
    )
    shape = dict(mesh.shape)
    body = halves if (shape["seq"], shape["ch"]) == (SEQ, CH) else any_mesh
    return jax.shard_map(
        body, mesh=mesh, in_specs=placed, out_specs=P(("seq", "ch"), None), check_vma=False
    )
```

```python
import functools
import math

import jax
import jax.numpy as jnp
import numpy as np
from jax import lax
from jax.experimental import pallas as pl
from jax.experimental.pallas import tpu as pltpu
from jax.sharding import PartitionSpec as P

highest = lax.Precision.HIGHEST
LANES = 128
MIB = 1 << 20


def phase_table(first, second, modulus):
    turns = first[:, None] * second[None, :] % modulus
    angles = turns.astype(jnp.float32) * (2.0 * math.pi / modulus)
    return (jnp.cos(angles), jnp.sin(angles))


def convolve(product, spectrum):
    seq_count = lax.axis_size("seq")
    tokens, width = product.shape
    length_two = 2 * seq_count * tokens
    offsets = jnp.arange(2 * seq_count, dtype=jnp.int32)
    places = jnp.arange(seq_count, dtype=jnp.int32)
    residues = jnp.arange(tokens, dtype=jnp.int32)
    off_cos, off_sin = phase_table(offsets, places, 2 * seq_count)
    res_cos, res_sin = phase_table(residues, residues, tokens)
    block = tokens // seq_count
    device = lax.axis_index("seq")
    pieces = lax.all_to_all(
        product.reshape(1, tokens, width), "seq", split_axis=1, concat_axis=0, tiled=True
    )
    values = pieces.astype(jnp.float32)
    real_part = jnp.einsum("kp,prc->krc", off_cos, values, precision=highest)
    imag_part = -jnp.einsum("kp,prc->krc", off_sin, values, precision=highest)
    own_rows = device * block + jnp.arange(block, dtype=jnp.int32)
    tw_cos, tw_sin = phase_table(offsets, own_rows, length_two)
    tw_cos = tw_cos[:, :, None]
    tw_sin = tw_sin[:, :, None]
    real_part, imag_part = (
        real_part * tw_cos + imag_part * tw_sin,
        imag_part * tw_cos - real_part * tw_sin,
    )
    real_part, imag_part = (
        lax.all_to_all(real_part, "seq", split_axis=0, concat_axis=1, tiled=True),
        lax.all_to_all(imag_part, "seq", split_axis=0, concat_axis=1, tiled=True),
    )
    real_next = jnp.einsum("grc,rs->gsc", real_part, res_cos, precision=highest) + jnp.einsum(
        "grc,rs->gsc", imag_part, res_sin, precision=highest
    )
    imag_next = jnp.einsum("grc,rs->gsc", imag_part, res_cos, precision=highest) - jnp.einsum(
        "grc,rs->gsc", real_part, res_sin, precision=highest
    )
    spec_real = spectrum[0]
    spec_imag = spectrum[1]
    real_part = real_next * spec_real - imag_next * spec_imag
    imag_part = real_next * spec_imag + imag_next * spec_real
    real_next = jnp.einsum("gsc,sr->grc", real_part, res_cos, precision=highest) - jnp.einsum(
        "gsc,sr->grc", imag_part, res_sin, precision=highest
    )
    imag_next = jnp.einsum("gsc,sr->grc", imag_part, res_cos, precision=highest) + jnp.einsum(
        "gsc,sr->grc", real_part, res_sin, precision=highest
    )
    own_offsets = 2 * device + jnp.arange(2, dtype=jnp.int32)
    un_cos, un_sin = phase_table(own_offsets, residues, length_two)
    un_cos = un_cos[:, :, None]
    un_sin = un_sin[:, :, None]
    real_part = real_next * un_cos - imag_next * un_sin
    imag_part = imag_next * un_cos + real_next * un_sin
    real_part, imag_part = (
        lax.all_to_all(real_part, "seq", split_axis=1, concat_axis=0, tiled=True),
        lax.all_to_all(imag_part, "seq", split_axis=1, concat_axis=0, tiled=True),
    )
    field = jnp.einsum("kp,krc->prc", off_cos, real_part, precision=highest) - jnp.einsum(
        "kp,krc->prc", off_sin, imag_part, precision=highest
    )
    field = field / length_two
    field = lax.all_to_all(field, "seq", split_axis=0, concat_axis=1, tiled=True)
    return field.reshape(tokens, width)


def any_mesh(gate_rows, key_rows, value_rows, spectrum, skip_bias):
    own = (key_rows.astype(jnp.float32) * value_rows.astype(jnp.float32)).astype(jnp.bfloat16)
    product = lax.all_to_all(own, "ch", split_axis=1, concat_axis=0, tiled=True)
    field = convolve(product, spectrum)
    field = lax.all_to_all(field, "ch", split_axis=0, concat_axis=1, tiled=True)
    gated = gate_rows.astype(jnp.float32) * (
        field + skip_bias[None, :] * own.astype(jnp.float32)
    )
    return gated.astype(jnp.bfloat16)


SEQ, CH, HALF = 8, 4, 4
DEVICES = SEQ * CH
ROOT = math.sqrt(0.5)
EARLY, LATE = (0, 1, 3), (2,)
NEAR = 64
VMEM = pl.BlockSpec(memory_space=pltpu.VMEM)
SMEM = pl.BlockSpec(memory_space=pltpu.SMEM)
STEP = 16


def swap(array, axis, mask, count):
    return lax.ppermute(array, axis, [(i, i ^ mask) for i in range(count)])


def columns_of(device):
    seq, ch = divmod(device, CH)
    return pl.ds((ch * HALF + seq % HALF) * LANES, LANES)


def rows_at(index, first=0):
    return pl.ds(pl.multiple_of(first + index * STEP, STEP), STEP)


def times(a, b):
    return a[0] * b[0] - a[1] * b[1], a[0] * b[1] + a[1] * b[0]


def root_16(power):
    return math.cos(power * math.pi / 8), math.sin(power * math.pi / 8)


def product_kernel(key_hbm, value_hbm, out_ref, key, value, sems):
    groups = DEVICES // 2
    width = key.shape[1] // CH
    copies = []
    for ch in range(CH):
        at = pl.ds(ch * width, width)
        copies.append(
            [
                pltpu.make_async_copy(source.at[:, at], to.at[:, at], sems.at[which, ch])
                for which, (source, to) in enumerate(((key_hbm, key), (value_hbm, value)))
            ]
        )
        for copy in copies[-1]:
            copy.start()
    for ch in range(CH):
        for copy in copies[ch]:
            copy.wait()
        for member in range(HALF):
            device = member * CH + ch
            at = columns_of(device)
            product = (key[:, at].astype(jnp.float32) * value[:, at].astype(jnp.float32)).astype(jnp.bfloat16)
            out_ref[device] = product
            out_ref[device + groups] = product


def spectrum_kernel(place_ref, *refs):
    count = len(refs) // 2
    spec, members = refs[:count], refs[count:]
    rows = members[0].shape[3]
    for member in range(count):
        for part in range(2):
            for odd in range(2):
                for bit in range(2):
                    values = spec[member][part, odd, pl.ds(bit, rows, stride=2), :]
                    members[member][part, odd, bit] = values.astype(jnp.bfloat16)


def members_of(spectrum, which, steps=4):
    size = spectrum.shape[2]
    piece = size // steps
    place = (lax.axis_index("seq") % HALF).astype(jnp.int32).reshape(1)
    spec_blocks = [
        pl.BlockSpec((2, 2, piece, LANES), lambda i, place, member=member: (0, 0, i, place[0] ^ member))
        for member in which
    ]
    return pl.pallas_call(
        spectrum_kernel,
        grid_spec=pltpu.PrefetchScalarGridSpec(
            num_scalar_prefetch=1,
            grid=(steps,),
            in_specs=spec_blocks,
            out_specs=[pl.BlockSpec((2, 2, 2, piece // 2, LANES), lambda i, place: (0, 0, 0, i, 0))] * len(which),
        ),
        out_shape=[jax.ShapeDtypeStruct((2, 2, 2, size // 2, LANES), jnp.bfloat16)] * len(which),
        compiler_params=pltpu.CompilerParams(vmem_limit_bytes=56 * MIB),
        name="spectrum",
    )(place, *[spectrum] * len(which))


def four_real(a0, a1, a2, a3):
    even, odd = a0 + a2, a1 + a3
    less, more = (a1 - a3) * ROOT, odd * ROOT
    return (
        (even + odd, None),
        (a0 + less, -(a2 + more)),
        (a0 - a2, a3 - a1),
        (a0 - less, a2 - more),
        (even - odd, None),
    )


def residues_of(values, sign):
    even = four_real(*values[0::2])
    odd = four_real(*[v * sign for v in values[1::2]])
    out = [None] * SEQ
    out[0] = (even[0][0] + odd[0][0], None)
    out[4] = (even[4][0], -odd[4][0])
    for j in (1, 2, 3):
        turned = times(odd[j], root_16(-j))
        out[j] = (even[j][0] + turned[0], even[j][1] + turned[1])
        out[8 - j] = (even[j][0] - turned[0], turned[1] - even[j][1])
    return out


def four_back(zero, four, one, two, three):
    plus, minus = zero + four, zero - four
    half_way = (one[0] - three[0]) * ROOT
    across = (one[1] + three[1]) * ROOT
    return (
        plus + two[0] + (one[0] + three[0]),
        minus - two[1] + (half_way - across),
        plus - two[0] + (three[1] - one[1]),
        minus + two[1] - (half_way + across),
    )


def blocks_of(parts):
    sums, turned = [], []
    for j in (1, 2, 3):
        a, b = parts[j], parts[8 - j]
        sums.append((a[0] + b[0], a[1] - b[1]))
        turned.append(times((a[0] - b[0], a[1] + b[1]), root_16(j)))
    even = four_back(parts[0][0], parts[4][0], *sums)
    odd = four_back(parts[0][0], -parts[4][1], *turned)
    return [value for pair in zip(even, odd) for value in pair]


def sign_of_half():
    return jnp.where(lax.axis_index("seq") < HALF, 1.0, -1.0).astype(jnp.float32)


def turn_table(size):
    angles = np.arange(2 * SEQ)[:, None] * np.arange(size)[None, :] * (2.0 * np.pi / (2 * SEQ * size))
    angles = angles.reshape(2, SEQ, size)
    between = np.broadcast_to(np.arange(size) * (2.0 * np.pi / size), (2, 1, size))
    angles = np.concatenate([angles, between], axis=1)
    table = np.stack([np.cos(angles), np.sin(angles)], axis=2).astype(np.float32)
    return jnp.asarray(np.repeat(table[..., None], LANES, axis=-1))


def split_table(size):
    turns = np.arange(2 * SEQ).reshape(2, SEQ) / (2 * SEQ * size)
    turns = 2 * np.pi * np.concatenate([turns, np.full((2, 1), 1 / size)], axis=1)
    near, far = (turns[:, :, None] * tokens for tokens in (np.arange(NEAR), np.arange(0, size, NEAR)))
    near = np.repeat(np.stack([np.cos(near), np.sin(near)], axis=2)[..., None], LANES, axis=-1)
    far = np.stack([np.cos(far), np.sin(far)], axis=3).reshape(-1)
    return jnp.asarray(near, jnp.float32), jnp.asarray(far, jnp.float32)


def forward_kernel(tokens, near, far, dft_ref, re_ref, im_ref, stage):
    half = lax.axis_index("seq") // HALF
    sign = sign_of_half()
    size = tokens.shape[1]
    short = size // 2
    chunks = NEAR // STEP

    def twiddle(j, a, at):
        index = ((half * (SEQ + 1) + j) * (size // NEAR) + a) * 2
        return times((near[j, 0, at, :], near[j, 1, at, :]), (far[index], far[index + 1]))

    def rows_of(index, carry):
        a = index // chunks
        near_at = rows_at(index % chunks)
        both = []
        for late in range(2):
            at = rows_at(index, late * short)
            parts = residues_of([tokens[p, at, :].astype(jnp.float32) for p in range(SEQ)], sign)
            turned = []
            for j, (real, imag) in enumerate(parts):
                cos, sin = twiddle(j, a + late * (short // NEAR), near_at)
                if imag is None:
                    turned.append((real * cos, -(real * sin)))
                else:
                    turned.append((real * cos + imag * sin, imag * cos - real * sin))
            both.append(turned)
        at = rows_at(index)
        cos, sin = twiddle(SEQ, a, near_at)
        for j in range(SEQ):
            x, y = both[0][j], both[1][j]
            less = x[0] - y[0], x[1] - y[1]
            pair = (x[0] + y[0], x[1] + y[1]), (less[0] * cos + less[1] * sin, less[1] * cos - less[0] * sin)
            for bit, (real, imag) in enumerate(pair):
                to = pl.ds((bit * SEQ + j) * LANES, LANES)
                real = real.astype(jnp.bfloat16)
                stage[at, to] = real
                stage[rows_at(index, short), to] = imag.astype(jnp.bfloat16)
                stage[rows_at(index, size), to] = -real
        return carry

    lax.fori_loop(0, short // STEP, rows_of, 0, unroll=2)
    re_ref[...] = jnp.dot(dft_ref[...], stage[pl.ds(0, size), :], preferred_element_type=jnp.float32)
    im_ref[...] = jnp.dot(dft_ref[...], stage[pl.ds(short, size), :], preferred_element_type=jnp.float32)


def filter_members(members, spec, re_ref, im_ref, dft_ref, back_re, back_im, stage):
    place = lax.axis_index("seq") % HALF
    short = re_ref.shape[0]
    size = 2 * short
    for index, member in enumerate(members):
        for odd in range(2):
            for bit in range(2):
                column = bit * SEQ + 2 * (place ^ member) + odd
                at = pl.ds(pl.multiple_of(column * LANES, LANES), LANES)
                h = spec[index][0, odd, bit].astype(jnp.float32), spec[index][1, odd, bit].astype(jnp.float32)
                y_re, y_im = times((re_ref[:, at], im_ref[:, at]), h)
                y_re, y_im = y_re.astype(jnp.bfloat16), y_im.astype(jnp.bfloat16)
                to = pl.ds((odd * 2 + bit) * LANES, LANES)
                stage[index, pl.ds(0, short), to] = y_im
                stage[index, pl.ds(short, short), to] = y_re
                stage[index, pl.ds(size, short), to] = -y_im
        back_im[place ^ member] = jnp.dot(
            dft_ref[...], stage[index, pl.ds(0, size), :], preferred_element_type=jnp.float32
        )
        back_re[place ^ member] = jnp.dot(
            dft_ref[...], stage[index, pl.ds(short, size), :], preferred_element_type=jnp.float32
        )


def early_kernel(*refs):
    spec, (re_ref, im_ref, dft_ref, back_re, back_im, stage) = refs[: len(EARLY)], refs[len(EARLY) :]
    filter_members(EARLY, spec, re_ref, im_ref, dft_ref, back_re, back_im, stage)


def late_kernel(*refs):
    spec, refs = refs[: len(LATE)], refs[len(LATE) :]
    early_re, early_im, re_ref, im_ref, table, dft_ref, out_ref, back_re, back_im, stage = refs
    sign = sign_of_half()
    place = lax.axis_index("seq") % HALF
    short = re_ref.shape[0]
    size = 2 * short
    filter_members(LATE, spec, re_ref, im_ref, dft_ref, back_re, back_im, stage)
    for member in EARLY:
        back_re[place ^ member] = early_re[place ^ member]
        back_im[place ^ member] = early_im[place ^ member]
    scale = 1.0 / (2 * SEQ * size)

    def rows_of(index, carry):
        at = rows_at(index)
        late = rows_at(index, short)
        cos, sin = table[SEQ, 0, at, :], table[SEQ, 1, at, :]
        parts = [], []
        for j in range(SEQ):
            pair = []
            for bit in range(2):
                to = pl.ds((j % 2 * 2 + bit) * LANES, LANES)
                pair.append((back_re[j // 2, at, to], back_im[j // 2, at, to]))
            a, b = pair[0], times(pair[1], (cos, sin))
            parts[0].append(times((a[0] + b[0], a[1] + b[1]), (table[j, 0, at, :], table[j, 1, at, :])))
            parts[1].append(times((a[0] - b[0], a[1] - b[1]), (table[j, 0, late, :], table[j, 1, late, :])))
        for where, values in zip((at, late), parts):
            for p, value in enumerate(blocks_of(values)):
                out_ref[p, where, :] = (value * (scale * sign if p % 2 else scale)).astype(jnp.bfloat16)
        return carry

    lax.fori_loop(0, short // STEP, rows_of, 0, unroll=2)


def table_kernel(member, table_hbm, near_hbm, table, near, out_ref, held, sems):
    half = lax.axis_index("seq") // HALF
    copies = [
        pltpu.make_async_copy(source.at[half], to, sems.at[index])
        for index, (source, to) in enumerate(((table_hbm, table), (near_hbm, near)))
    ]
    for copy in copies:
        copy.start()
    rows = out_ref.shape[3]
    for part in range(2):
        for odd in range(2):
            held[...] = member[part, odd].astype(jnp.float32)
            for bit in range(2):
                out_ref[part, odd, bit] = held[pl.ds(bit, rows, stride=2), :].astype(jnp.bfloat16)
    for copy in copies:
        copy.wait()


def gate_kernel(gate_ref, key_ref, value_ref, skip_ref, field_ref, out_hbm, held, sems):
    copies = []
    for ch in range(CH):
        for member in range(HALF):
            device = member * CH + ch
            at = columns_of(device)
            product = (key_ref[:, at].astype(jnp.float32) * value_ref[:, at].astype(jnp.float32)).astype(jnp.bfloat16)
            field = field_ref[device].astype(jnp.float32) + field_ref[device + DEVICES // 2].astype(jnp.float32)
            gated = gate_ref[:, at].astype(jnp.float32) * (field + skip_ref[:, at] * product.astype(jnp.float32))
            held[:, at] = gated.astype(jnp.bfloat16)
        columns = pl.ds(ch * HALF * LANES, HALF * LANES)
        copies.append(pltpu.make_async_copy(held.at[:, columns], out_hbm.at[:, columns], sems.at[ch]))
        copies[-1].start()
    for copy in copies:
        copy.wait()


def call(kernel, name, ins, outs, scratch=(), limit=24 * MIB, hbm=(), cost=None, aliases=None, to_hbm=False):
    return pl.pallas_call(
        kernel,
        out_shape=tuple(jax.ShapeDtypeStruct(shape, dtype) for shape, dtype in outs),
        in_specs=[pl.BlockSpec(memory_space=pl.ANY) if index in hbm else SMEM if x.ndim == 1 else VMEM for index, x in enumerate(ins)],
        out_specs=tuple(pl.BlockSpec(memory_space=pl.ANY) if to_hbm else VMEM for _ in outs),
        scratch_shapes=list(scratch),
        compiler_params=pltpu.CompilerParams(vmem_limit_bytes=limit),
        cost_estimate=cost,
        input_output_aliases=aliases or {},
        name=name,
    )(*ins)


def halves(gate_rows, key_rows, value_rows, spectrum, skip_bias):
    bf16, f32 = jnp.bfloat16, jnp.float32
    rows, channels = key_rows.shape
    size = rows * CH
    short = size // 2
    everywhere = ("seq", "ch")

    angles = np.arange(short)[:, None] * np.arange(short)[None, :] % short * (2.0 * np.pi / short)
    dft = jnp.asarray(np.concatenate([np.cos(angles), np.sin(angles)], axis=1), bf16)
    table = turn_table(size)
    near, far = split_table(size)

    sends = call(
        product_kernel,
        "product",
        [key_rows, value_rows],
        [((DEVICES, rows, LANES), bf16)],
        [pltpu.VMEM((rows, channels), bf16)] * 2 + [pltpu.SemaphoreType.DMA((2, CH))],
        limit=56 * MIB,
        hbm=(0, 1),
    )[0]
    opposite = lax.axis_index("seq") % HALF ^ 3
    last = lax.dynamic_slice_in_dim(spectrum, opposite * LANES, LANES, axis=3).astype(bf16)
    last = swap(last, "seq", 3, SEQ)
    cost = pl.CostEstimate(flops=40000000000, bytes_accessed=1 << 20, transcendentals=0)
    table, near, last = call(
        table_kernel,
        "table",
        [last, table, near],
        [(table.shape[1:], f32), (near.shape[1:], f32), ((2, 2, 2, short, LANES), bf16)],
        [pltpu.VMEM((size, LANES), f32), pltpu.SemaphoreType.DMA((2,))],
        hbm=(1, 2),
        cost=cost,
    )
    spec = members_of(spectrum, (0, 1, 2))
    tokens = lax.all_to_all(sends, everywhere, split_axis=0, concat_axis=0, tiled=True).reshape(SEQ, size, LANES)
    spec = [spec[0]] + [swap(spec[member], "seq", member, SEQ) for member in (1, 2)] + [last]
    freq = call(
        forward_kernel,
        "forward",
        [tokens, near, far, dft],
        [((short, 2 * SEQ * LANES), f32)] * 2,
        [pltpu.VMEM((3 * short, 2 * SEQ * LANES), bf16)],
    )
    back = ((HALF, short, 4 * LANES), f32)
    early = call(
        early_kernel,
        "early_members",
        [*[spec[member] for member in EARLY], *freq, dft],
        [back] * 2,
        [pltpu.VMEM((len(EARLY), 3 * short, 4 * LANES), bf16)],
    )
    shares = call(
        late_kernel,
        "late_member",
        [*[spec[member] for member in LATE], *early, *freq, table, dft],
        [((SEQ, size, LANES), bf16)],
        [pltpu.VMEM(*back)] * 2 + [pltpu.VMEM((len(LATE), 3 * short, 4 * LANES), bf16)],
    )[0].reshape(DEVICES, rows, LANES)
    field = lax.all_to_all(shares, everywhere, split_axis=0, concat_axis=0, tiled=True)
    return call(
        gate_kernel,
        "gate",
        [gate_rows, key_rows, value_rows, skip_bias.reshape(1, channels), field],
        [((rows, channels), bf16)],
        [pltpu.VMEM((rows, channels), bf16), pltpu.SemaphoreType.DMA((CH,))],
        to_hbm=True,
    )[0]


def solution(mesh):
    placed = (
        P(("seq", "ch"), None),
        P(("seq", "ch"), None),
        P(("seq", "ch"), None),
        P(None, "seq", None, "ch"),
        P(),
    )
    shape = dict(mesh.shape)
    body = halves if (shape["seq"], shape["ch"]) == (SEQ, CH) else any_mesh
    return jax.shard_map(
        body, mesh=mesh, in_specs=placed, out_specs=P(("seq", "ch"), None), check_vma=False
    )
```

```python
import functools
import math

import jax
import jax.numpy as jnp
import numpy as np
from jax import lax
from jax.experimental import pallas as pl
from jax.experimental.pallas import tpu as pltpu
from jax.sharding import PartitionSpec as P

highest = lax.Precision.HIGHEST
LANES = 128
MIB = 1 << 20


def phase_table(first, second, modulus):
    turns = first[:, None] * second[None, :] % modulus
    angles = turns.astype(jnp.float32) * (2.0 * math.pi / modulus)
    return (jnp.cos(angles), jnp.sin(angles))


def convolve(product, spectrum):
    seq_count = lax.axis_size("seq")
    tokens, width = product.shape
    length_two = 2 * seq_count * tokens
    offsets = jnp.arange(2 * seq_count, dtype=jnp.int32)
    places = jnp.arange(seq_count, dtype=jnp.int32)
    residues = jnp.arange(tokens, dtype=jnp.int32)
    off_cos, off_sin = phase_table(offsets, places, 2 * seq_count)
    res_cos, res_sin = phase_table(residues, residues, tokens)
    block = tokens // seq_count
    device = lax.axis_index("seq")
    pieces = lax.all_to_all(
        product.reshape(1, tokens, width), "seq", split_axis=1, concat_axis=0, tiled=True
    )
    values = pieces.astype(jnp.float32)
    real_part = jnp.einsum("kp,prc->krc", off_cos, values, precision=highest)
    imag_part = -jnp.einsum("kp,prc->krc", off_sin, values, precision=highest)
    own_rows = device * block + jnp.arange(block, dtype=jnp.int32)
    tw_cos, tw_sin = phase_table(offsets, own_rows, length_two)
    tw_cos = tw_cos[:, :, None]
    tw_sin = tw_sin[:, :, None]
    real_part, imag_part = (
        real_part * tw_cos + imag_part * tw_sin,
        imag_part * tw_cos - real_part * tw_sin,
    )
    real_part, imag_part = (
        lax.all_to_all(real_part, "seq", split_axis=0, concat_axis=1, tiled=True),
        lax.all_to_all(imag_part, "seq", split_axis=0, concat_axis=1, tiled=True),
    )
    real_next = jnp.einsum("grc,rs->gsc", real_part, res_cos, precision=highest) + jnp.einsum(
        "grc,rs->gsc", imag_part, res_sin, precision=highest
    )
    imag_next = jnp.einsum("grc,rs->gsc", imag_part, res_cos, precision=highest) - jnp.einsum(
        "grc,rs->gsc", real_part, res_sin, precision=highest
    )
    spec_real = spectrum[0]
    spec_imag = spectrum[1]
    real_part = real_next * spec_real - imag_next * spec_imag
    imag_part = real_next * spec_imag + imag_next * spec_real
    real_next = jnp.einsum("gsc,sr->grc", real_part, res_cos, precision=highest) - jnp.einsum(
        "gsc,sr->grc", imag_part, res_sin, precision=highest
    )
    imag_next = jnp.einsum("gsc,sr->grc", imag_part, res_cos, precision=highest) + jnp.einsum(
        "gsc,sr->grc", real_part, res_sin, precision=highest
    )
    own_offsets = 2 * device + jnp.arange(2, dtype=jnp.int32)
    un_cos, un_sin = phase_table(own_offsets, residues, length_two)
    un_cos = un_cos[:, :, None]
    un_sin = un_sin[:, :, None]
    real_part = real_next * un_cos - imag_next * un_sin
    imag_part = imag_next * un_cos + real_next * un_sin
    real_part, imag_part = (
        lax.all_to_all(real_part, "seq", split_axis=1, concat_axis=0, tiled=True),
        lax.all_to_all(imag_part, "seq", split_axis=1, concat_axis=0, tiled=True),
    )
    field = jnp.einsum("kp,krc->prc", off_cos, real_part, precision=highest) - jnp.einsum(
        "kp,krc->prc", off_sin, imag_part, precision=highest
    )
    field = field / length_two
    field = lax.all_to_all(field, "seq", split_axis=0, concat_axis=1, tiled=True)
    return field.reshape(tokens, width)


def any_mesh(gate_rows, key_rows, value_rows, spectrum, skip_bias):
    own = (key_rows.astype(jnp.float32) * value_rows.astype(jnp.float32)).astype(jnp.bfloat16)
    product = lax.all_to_all(own, "ch", split_axis=1, concat_axis=0, tiled=True)
    field = convolve(product, spectrum)
    field = lax.all_to_all(field, "ch", split_axis=0, concat_axis=1, tiled=True)
    gated = gate_rows.astype(jnp.float32) * (
        field + skip_bias[None, :] * own.astype(jnp.float32)
    )
    return gated.astype(jnp.bfloat16)


SEQ, CH, HALF = 8, 4, 4
DEVICES = SEQ * CH
ROOT = math.sqrt(0.5)
EARLY, LATE = (0, 1, 3), (2,)
NEAR = 64
VMEM = pl.BlockSpec(memory_space=pltpu.VMEM)
SMEM = pl.BlockSpec(memory_space=pltpu.SMEM)
STEP = 16


def swap(array, axis, mask, count):
    return lax.ppermute(array, axis, [(i, i ^ mask) for i in range(count)])


def columns_of(device):
    seq, ch = divmod(device, CH)
    return pl.ds((ch * HALF + seq % HALF) * LANES, LANES)


def rows_at(index, first=0):
    return pl.ds(pl.multiple_of(first + index * STEP, STEP), STEP)


def times(a, b):
    return a[0] * b[0] - a[1] * b[1], a[0] * b[1] + a[1] * b[0]


def root_16(power):
    return math.cos(power * math.pi / 8), math.sin(power * math.pi / 8)


def product_kernel(key_hbm, value_hbm, out_ref, key, value, sems):
    groups = DEVICES // 2
    width = key.shape[1] // CH
    copies = []
    for ch in range(CH):
        at = pl.ds(ch * width, width)
        copies.append(
            [
                pltpu.make_async_copy(source.at[:, at], to.at[:, at], sems.at[which, ch])
                for which, (source, to) in enumerate(((key_hbm, key), (value_hbm, value)))
            ]
        )
        for copy in copies[-1]:
            copy.start()
    for ch in range(CH):
        for copy in copies[ch]:
            copy.wait()
        for member in range(HALF):
            device = member * CH + ch
            at = columns_of(device)
            product = (key[:, at].astype(jnp.float32) * value[:, at].astype(jnp.float32)).astype(jnp.bfloat16)
            out_ref[device] = product
            out_ref[device + groups] = product


def spectrum_kernel(place_ref, *refs):
    count = len(refs) // 2
    spec, members = refs[:count], refs[count:]
    rows = members[0].shape[3]
    for member in range(count):
        for part in range(2):
            for odd in range(2):
                for bit in range(2):
                    values = spec[member][part, odd, pl.ds(bit, rows, stride=2), :]
                    members[member][part, odd, bit] = values.astype(jnp.bfloat16)


def members_of(spectrum, which, steps=4):
    size = spectrum.shape[2]
    piece = size // steps
    place = (lax.axis_index("seq") % HALF).astype(jnp.int32).reshape(1)
    spec_blocks = [
        pl.BlockSpec((2, 2, piece, LANES), lambda i, place, member=member: (0, 0, i, place[0] ^ member))
        for member in which
    ]
    return pl.pallas_call(
        spectrum_kernel,
        grid_spec=pltpu.PrefetchScalarGridSpec(
            num_scalar_prefetch=1,
            grid=(steps,),
            in_specs=spec_blocks,
            out_specs=[pl.BlockSpec((2, 2, 2, piece // 2, LANES), lambda i, place: (0, 0, 0, i, 0))] * len(which),
        ),
        out_shape=[jax.ShapeDtypeStruct((2, 2, 2, size // 2, LANES), jnp.bfloat16)] * len(which),
        compiler_params=pltpu.CompilerParams(vmem_limit_bytes=56 * MIB),
        name="spectrum",
    )(place, *[spectrum] * len(which))


def four_real(a0, a1, a2, a3):
    even, odd = a0 + a2, a1 + a3
    less, more = (a1 - a3) * ROOT, odd * ROOT
    return (
        (even + odd, None),
        (a0 + less, -(a2 + more)),
        (a0 - a2, a3 - a1),
        (a0 - less, a2 - more),
        (even - odd, None),
    )


def residues_of(values, sign):
    even = four_real(*values[0::2])
    odd = four_real(*[v * sign for v in values[1::2]])
    out = [None] * SEQ
    out[0] = (even[0][0] + odd[0][0], None)
    out[4] = (even[4][0], -odd[4][0])
    for j in (1, 2, 3):
        turned = times(odd[j], root_16(-j))
        out[j] = (even[j][0] + turned[0], even[j][1] + turned[1])
        out[8 - j] = (even[j][0] - turned[0], turned[1] - even[j][1])
    return out


def four_back(zero, four, one, two, three):
    plus, minus = zero + four, zero - four
    half_way = (one[0] - three[0]) * ROOT
    across = (one[1] + three[1]) * ROOT
    return (
        plus + two[0] + (one[0] + three[0]),
        minus - two[1] + (half_way - across),
        plus - two[0] + (three[1] - one[1]),
        minus + two[1] - (half_way + across),
    )


def blocks_of(parts):
    sums, turned = [], []
    for j in (1, 2, 3):
        a, b = parts[j], parts[8 - j]
        sums.append((a[0] + b[0], a[1] - b[1]))
        turned.append(times((a[0] - b[0], a[1] + b[1]), root_16(j)))
    even = four_back(parts[0][0], parts[4][0], *sums)
    odd = four_back(parts[0][0], -parts[4][1], *turned)
    return [value for pair in zip(even, odd) for value in pair]


def sign_of_half():
    return jnp.where(lax.axis_index("seq") < HALF, 1.0, -1.0).astype(jnp.float32)


def turn_table(size):
    angles = np.arange(2 * SEQ)[:, None] * np.arange(size)[None, :] * (2.0 * np.pi / (2 * SEQ * size))
    angles = angles.reshape(2, SEQ, size)
    between = np.broadcast_to(np.arange(size) * (2.0 * np.pi / size), (2, 1, size))
    angles = np.concatenate([angles, between], axis=1)
    table = np.stack([np.cos(angles), np.sin(angles)], axis=2).astype(np.float32)
    return jnp.asarray(np.repeat(table[..., None], LANES, axis=-1))


def split_table(size):
    turns = np.arange(2 * SEQ).reshape(2, SEQ) / (2 * SEQ * size)
    turns = 2 * np.pi * np.concatenate([turns, np.full((2, 1), 1 / size)], axis=1)
    near, far = (turns[:, :, None] * tokens for tokens in (np.arange(NEAR), np.arange(0, size, NEAR)))
    near = np.repeat(np.stack([np.cos(near), np.sin(near)], axis=2)[..., None], LANES, axis=-1)
    far = np.stack([np.cos(far), np.sin(far)], axis=3).reshape(-1)
    return jnp.asarray(near, jnp.float32), jnp.asarray(far, jnp.float32)


def forward_kernel(tokens, near, far, dft_ref, re_ref, im_ref, stage):
    half = lax.axis_index("seq") // HALF
    sign = sign_of_half()
    size = tokens.shape[1]
    short = size // 2
    chunks = NEAR // STEP

    def twiddle(j, a, at):
        index = ((half * (SEQ + 1) + j) * (size // NEAR) + a) * 2
        return times((near[j, 0, at, :], near[j, 1, at, :]), (far[index], far[index + 1]))

    def rows_of(index, carry):
        a = index // chunks
        near_at = rows_at(index % chunks)
        both = []
        for late in range(2):
            at = rows_at(index, late * short)
            parts = residues_of([tokens[p, at, :].astype(jnp.float32) for p in range(SEQ)], sign)
            turned = []
            for j, (real, imag) in enumerate(parts):
                cos, sin = twiddle(j, a + late * (short // NEAR), near_at)
                if imag is None:
                    turned.append((real * cos, -(real * sin)))
                else:
                    turned.append((real * cos + imag * sin, imag * cos - real * sin))
            both.append(turned)
        at = rows_at(index)
        cos, sin = twiddle(SEQ, a, near_at)
        for j in range(SEQ):
            x, y = both[0][j], both[1][j]
            less = x[0] - y[0], x[1] - y[1]
            pair = (x[0] + y[0], x[1] + y[1]), (less[0] * cos + less[1] * sin, less[1] * cos - less[0] * sin)
            for bit, (real, imag) in enumerate(pair):
                to = pl.ds((bit * SEQ + j) * LANES, LANES)
                real = real.astype(jnp.bfloat16)
                stage[at, to] = real
                stage[rows_at(index, short), to] = imag.astype(jnp.bfloat16)
                stage[rows_at(index, size), to] = -real
        return carry

    lax.fori_loop(0, short // STEP, rows_of, 0, unroll=2)
    re_ref[...] = jnp.dot(dft_ref[...], stage[pl.ds(0, size), :], preferred_element_type=jnp.float32)
    im_ref[...] = jnp.dot(dft_ref[...], stage[pl.ds(short, size), :], preferred_element_type=jnp.float32)


def filter_members(members, spec, re_ref, im_ref, dft_ref, back_re, back_im, stage):
    place = lax.axis_index("seq") % HALF
    short = re_ref.shape[0]
    size = 2 * short
    for index, member in enumerate(members):
        for odd in range(2):
            for bit in range(2):
                column = bit * SEQ + 2 * (place ^ member) + odd
                at = pl.ds(pl.multiple_of(column * LANES, LANES), LANES)
                h = spec[index][0, odd, bit].astype(jnp.float32), spec[index][1, odd, bit].astype(jnp.float32)
                y_re, y_im = times((re_ref[:, at], im_ref[:, at]), h)
                y_re, y_im = y_re.astype(jnp.bfloat16), y_im.astype(jnp.bfloat16)
                to = pl.ds((odd * 2 + bit) * LANES, LANES)
                stage[index, pl.ds(0, short), to] = y_im
                stage[index, pl.ds(short, short), to] = y_re
                stage[index, pl.ds(size, short), to] = -y_im
        back_im[place ^ member] = jnp.dot(
            dft_ref[...], stage[index, pl.ds(0, size), :], preferred_element_type=jnp.float32
        )
        back_re[place ^ member] = jnp.dot(
            dft_ref[...], stage[index, pl.ds(short, size), :], preferred_element_type=jnp.float32
        )


def early_kernel(*refs):
    spec, (re_ref, im_ref, dft_ref, back_re, back_im, stage) = refs[: len(EARLY)], refs[len(EARLY) :]
    filter_members(EARLY, spec, re_ref, im_ref, dft_ref, back_re, back_im, stage)


def late_kernel(*refs):
    spec, refs = refs[: len(LATE)], refs[len(LATE) :]
    early_re, early_im, re_ref, im_ref, table, dft_ref, out_ref, back_re, back_im, stage = refs
    sign = sign_of_half()
    place = lax.axis_index("seq") % HALF
    short = re_ref.shape[0]
    size = 2 * short
    filter_members(LATE, spec, re_ref, im_ref, dft_ref, back_re, back_im, stage)
    scale = 1.0 / (2 * SEQ * size)

    def rows_of(index, carry, last):
        at = rows_at(index)
        late = rows_at(index, short)
        cos, sin = table[SEQ, 0, at, :], table[SEQ, 1, at, :]
        parts = [], []
        for j in range(SEQ):
            pair = []
            for bit in range(2):
                to = pl.ds((j % 2 * 2 + bit) * LANES, LANES)
                pair.append(tuple(ref[j // 2, at, to] for ref in ((back_re, back_im) if j // 2 == last else (early_re, early_im))))
            a, b = pair[0], times(pair[1], (cos, sin))
            parts[0].append(times((a[0] + b[0], a[1] + b[1]), (table[j, 0, at, :], table[j, 1, at, :])))
            parts[1].append(times((a[0] - b[0], a[1] - b[1]), (table[j, 0, late, :], table[j, 1, late, :])))
        for where, values in zip((at, late), parts):
            for p, value in enumerate(blocks_of(values)):
                out_ref[p, where, :] = (value * (scale * sign if p % 2 else scale)).astype(jnp.bfloat16)
        return carry

    for own in range(HALF):

        @pl.when(place == own)
        def _(last=own ^ LATE[0]):
            lax.fori_loop(0, short // STEP, functools.partial(rows_of, last=last), 0, unroll=2)


def table_kernel(member, table_hbm, near_hbm, table, near, out_ref, held, sems):
    half = lax.axis_index("seq") // HALF
    copies = [
        pltpu.make_async_copy(source.at[half], to, sems.at[index])
        for index, (source, to) in enumerate(((table_hbm, table), (near_hbm, near)))
    ]
    for copy in copies:
        copy.start()
    rows = out_ref.shape[3]
    for part in range(2):
        for odd in range(2):
            held[...] = member[part, odd].astype(jnp.float32)
            for bit in range(2):
                out_ref[part, odd, bit] = held[pl.ds(bit, rows, stride=2), :].astype(jnp.bfloat16)
    for copy in copies:
        copy.wait()


def gate_kernel(gate_ref, key_ref, value_ref, skip_ref, field_ref, out_hbm, held, sems):
    copies = []
    for ch in range(CH):
        for member in range(HALF):
            device = member * CH + ch
            at = columns_of(device)
            product = (key_ref[:, at].astype(jnp.float32) * value_ref[:, at].astype(jnp.float32)).astype(jnp.bfloat16)
            field = field_ref[device].astype(jnp.float32) + field_ref[device + DEVICES // 2].astype(jnp.float32)
            gated = gate_ref[:, at].astype(jnp.float32) * (field + skip_ref[:, at] * product.astype(jnp.float32))
            held[:, at] = gated.astype(jnp.bfloat16)
        columns = pl.ds(ch * HALF * LANES, HALF * LANES)
        copies.append(pltpu.make_async_copy(held.at[:, columns], out_hbm.at[:, columns], sems.at[ch]))
        copies[-1].start()
    for copy in copies:
        copy.wait()


def call(kernel, name, ins, outs, scratch=(), limit=24 * MIB, hbm=(), cost=None, aliases=None, to_hbm=False):
    return pl.pallas_call(
        kernel,
        out_shape=tuple(jax.ShapeDtypeStruct(shape, dtype) for shape, dtype in outs),
        in_specs=[pl.BlockSpec(memory_space=pl.ANY) if index in hbm else SMEM if x.ndim == 1 else VMEM for index, x in enumerate(ins)],
        out_specs=tuple(pl.BlockSpec(memory_space=pl.ANY) if to_hbm else VMEM for _ in outs),
        scratch_shapes=list(scratch),
        compiler_params=pltpu.CompilerParams(vmem_limit_bytes=limit),
        cost_estimate=cost,
        input_output_aliases=aliases or {},
        name=name,
    )(*ins)


def halves(gate_rows, key_rows, value_rows, spectrum, skip_bias):
    bf16, f32 = jnp.bfloat16, jnp.float32
    rows, channels = key_rows.shape
    size = rows * CH
    short = size // 2
    everywhere = ("seq", "ch")

    angles = np.arange(short)[:, None] * np.arange(short)[None, :] % short * (2.0 * np.pi / short)
    dft = jnp.asarray(np.concatenate([np.cos(angles), np.sin(angles)], axis=1), bf16)
    table = turn_table(size)
    near, far = split_table(size)

    sends = call(
        product_kernel,
        "product",
        [key_rows, value_rows],
        [((DEVICES, rows, LANES), bf16)],
        [pltpu.VMEM((rows, channels), bf16)] * 2 + [pltpu.SemaphoreType.DMA((2, CH))],
        limit=56 * MIB,
        hbm=(0, 1),
    )[0]
    opposite = lax.axis_index("seq") % HALF ^ 3
    last = lax.dynamic_slice_in_dim(spectrum, opposite * LANES, LANES, axis=3).astype(bf16)
    last = swap(last, "seq", 3, SEQ)
    cost = pl.CostEstimate(flops=40000000000, bytes_accessed=1 << 20, transcendentals=0)
    table, near, last = call(
        table_kernel,
        "table",
        [last, table, near],
        [(table.shape[1:], f32), (near.shape[1:], f32), ((2, 2, 2, short, LANES), bf16)],
        [pltpu.VMEM((size, LANES), f32), pltpu.SemaphoreType.DMA((2,))],
        hbm=(1, 2),
        cost=cost,
    )
    spec = members_of(spectrum, (0, 1, 2))
    tokens = lax.all_to_all(sends, everywhere, split_axis=0, concat_axis=0, tiled=True).reshape(SEQ, size, LANES)
    spec = [spec[0]] + [swap(spec[member], "seq", member, SEQ) for member in (1, 2)] + [last]
    freq = call(
        forward_kernel,
        "forward",
        [tokens, near, far, dft],
        [((short, 2 * SEQ * LANES), f32)] * 2,
        [pltpu.VMEM((3 * short, 2 * SEQ * LANES), bf16)],
    )
    back = ((HALF, short, 4 * LANES), f32)
    early = call(
        early_kernel,
        "early_members",
        [*[spec[member] for member in EARLY], *freq, dft],
        [back] * 2,
        [pltpu.VMEM((len(EARLY), 3 * short, 4 * LANES), bf16)],
    )
    shares = call(
        late_kernel,
        "late_member",
        [*[spec[member] for member in LATE], *early, *freq, table, dft],
        [((SEQ, size, LANES), bf16)],
        [pltpu.VMEM(*back)] * 2 + [pltpu.VMEM((len(LATE), 3 * short, 4 * LANES), bf16)],
    )[0].reshape(DEVICES, rows, LANES)
    field = lax.all_to_all(shares, everywhere, split_axis=0, concat_axis=0, tiled=True)
    return call(
        gate_kernel,
        "gate",
        [gate_rows, key_rows, value_rows, skip_bias.reshape(1, channels), field],
        [((rows, channels), bf16)],
        [pltpu.VMEM((rows, channels), bf16), pltpu.SemaphoreType.DMA((CH,))],
        to_hbm=True,
    )[0]


def solution(mesh):
    placed = (
        P(("seq", "ch"), None),
        P(("seq", "ch"), None),
        P(("seq", "ch"), None),
        P(None, "seq", None, "ch"),
        P(),
    )
    shape = dict(mesh.shape)
    body = halves if (shape["seq"], shape["ch"]) == (SEQ, CH) else any_mesh
    return jax.shard_map(
        body, mesh=mesh, in_specs=placed, out_specs=P(("seq", "ch"), None), check_vma=False
    )
```

```python
import functools
import math

import jax
import jax.numpy as jnp
import numpy as np
from jax import lax
from jax.experimental import pallas as pl
from jax.experimental.pallas import tpu as pltpu
from jax.sharding import PartitionSpec as P

highest = lax.Precision.HIGHEST
LANES = 128
MIB = 1 << 20


def phase_table(first, second, modulus):
    turns = first[:, None] * second[None, :] % modulus
    angles = turns.astype(jnp.float32) * (2.0 * math.pi / modulus)
    return (jnp.cos(angles), jnp.sin(angles))


def convolve(product, spectrum):
    seq_count = lax.axis_size("seq")
    tokens, width = product.shape
    length_two = 2 * seq_count * tokens
    offsets = jnp.arange(2 * seq_count, dtype=jnp.int32)
    places = jnp.arange(seq_count, dtype=jnp.int32)
    residues = jnp.arange(tokens, dtype=jnp.int32)
    off_cos, off_sin = phase_table(offsets, places, 2 * seq_count)
    res_cos, res_sin = phase_table(residues, residues, tokens)
    block = tokens // seq_count
    device = lax.axis_index("seq")
    pieces = lax.all_to_all(
        product.reshape(1, tokens, width), "seq", split_axis=1, concat_axis=0, tiled=True
    )
    values = pieces.astype(jnp.float32)
    real_part = jnp.einsum("kp,prc->krc", off_cos, values, precision=highest)
    imag_part = -jnp.einsum("kp,prc->krc", off_sin, values, precision=highest)
    own_rows = device * block + jnp.arange(block, dtype=jnp.int32)
    tw_cos, tw_sin = phase_table(offsets, own_rows, length_two)
    tw_cos = tw_cos[:, :, None]
    tw_sin = tw_sin[:, :, None]
    real_part, imag_part = (
        real_part * tw_cos + imag_part * tw_sin,
        imag_part * tw_cos - real_part * tw_sin,
    )
    real_part, imag_part = (
        lax.all_to_all(real_part, "seq", split_axis=0, concat_axis=1, tiled=True),
        lax.all_to_all(imag_part, "seq", split_axis=0, concat_axis=1, tiled=True),
    )
    real_next = jnp.einsum("grc,rs->gsc", real_part, res_cos, precision=highest) + jnp.einsum(
        "grc,rs->gsc", imag_part, res_sin, precision=highest
    )
    imag_next = jnp.einsum("grc,rs->gsc", imag_part, res_cos, precision=highest) - jnp.einsum(
        "grc,rs->gsc", real_part, res_sin, precision=highest
    )
    spec_real = spectrum[0]
    spec_imag = spectrum[1]
    real_part = real_next * spec_real - imag_next * spec_imag
    imag_part = real_next * spec_imag + imag_next * spec_real
    real_next = jnp.einsum("gsc,sr->grc", real_part, res_cos, precision=highest) - jnp.einsum(
        "gsc,sr->grc", imag_part, res_sin, precision=highest
    )
    imag_next = jnp.einsum("gsc,sr->grc", imag_part, res_cos, precision=highest) + jnp.einsum(
        "gsc,sr->grc", real_part, res_sin, precision=highest
    )
    own_offsets = 2 * device + jnp.arange(2, dtype=jnp.int32)
    un_cos, un_sin = phase_table(own_offsets, residues, length_two)
    un_cos = un_cos[:, :, None]
    un_sin = un_sin[:, :, None]
    real_part = real_next * un_cos - imag_next * un_sin
    imag_part = imag_next * un_cos + real_next * un_sin
    real_part, imag_part = (
        lax.all_to_all(real_part, "seq", split_axis=1, concat_axis=0, tiled=True),
        lax.all_to_all(imag_part, "seq", split_axis=1, concat_axis=0, tiled=True),
    )
    field = jnp.einsum("kp,krc->prc", off_cos, real_part, precision=highest) - jnp.einsum(
        "kp,krc->prc", off_sin, imag_part, precision=highest
    )
    field = field / length_two
    field = lax.all_to_all(field, "seq", split_axis=0, concat_axis=1, tiled=True)
    return field.reshape(tokens, width)


def any_mesh(gate_rows, key_rows, value_rows, spectrum, skip_bias):
    own = (key_rows.astype(jnp.float32) * value_rows.astype(jnp.float32)).astype(jnp.bfloat16)
    product = lax.all_to_all(own, "ch", split_axis=1, concat_axis=0, tiled=True)
    field = convolve(product, spectrum)
    field = lax.all_to_all(field, "ch", split_axis=0, concat_axis=1, tiled=True)
    gated = gate_rows.astype(jnp.float32) * (
        field + skip_bias[None, :] * own.astype(jnp.float32)
    )
    return gated.astype(jnp.bfloat16)


SEQ, CH, HALF = 8, 4, 4
DEVICES = SEQ * CH
ROOT = math.sqrt(0.5)
EARLY, LATE = (0, 1, 3), (2,)
NEAR = 64
VMEM = pl.BlockSpec(memory_space=pltpu.VMEM)
SMEM = pl.BlockSpec(memory_space=pltpu.SMEM)
STEP = 16


def swap(array, axis, mask, count):
    return lax.ppermute(array, axis, [(i, i ^ mask) for i in range(count)])


def columns_of(device):
    seq, ch = divmod(device, CH)
    return pl.ds((ch * HALF + seq % HALF) * LANES, LANES)


def rows_at(index, first=0):
    return pl.ds(pl.multiple_of(first + index * STEP, STEP), STEP)


def times(a, b):
    return a[0] * b[0] - a[1] * b[1], a[0] * b[1] + a[1] * b[0]


def root_16(power):
    return math.cos(power * math.pi / 8), math.sin(power * math.pi / 8)


def product_kernel(key_hbm, value_hbm, out_ref, key, value, sems):
    groups = DEVICES // 2
    width = key.shape[1] // CH
    copies = []
    for ch in range(CH):
        at = pl.ds(ch * width, width)
        copies.append(
            [
                pltpu.make_async_copy(source.at[:, at], to.at[:, at], sems.at[which, ch])
                for which, (source, to) in enumerate(((key_hbm, key), (value_hbm, value)))
            ]
        )
        for copy in copies[-1]:
            copy.start()
    for ch in range(CH):
        for copy in copies[ch]:
            copy.wait()
        for member in range(HALF):
            device = member * CH + ch
            at = columns_of(device)
            product = (key[:, at].astype(jnp.float32) * value[:, at].astype(jnp.float32)).astype(jnp.bfloat16)
            out_ref[device] = product
            out_ref[device + groups] = product


def spectrum_kernel(place_ref, *refs):
    count = len(refs) // 2
    spec, members = refs[:count], refs[count:]
    rows = members[0].shape[3]
    for member in range(count):
        for part in range(2):
            for odd in range(2):
                for bit in range(2):
                    values = spec[member][part, odd, pl.ds(bit, rows, stride=2), :]
                    members[member][part, odd, bit] = values.astype(jnp.bfloat16)


def members_of(spectrum, which, steps=4):
    size = spectrum.shape[2]
    piece = size // steps
    place = (lax.axis_index("seq") % HALF).astype(jnp.int32).reshape(1)
    spec_blocks = [
        pl.BlockSpec((2, 2, piece, LANES), lambda i, place, member=member: (0, 0, i, place[0] ^ member))
        for member in which
    ]
    return pl.pallas_call(
        spectrum_kernel,
        grid_spec=pltpu.PrefetchScalarGridSpec(
            num_scalar_prefetch=1,
            grid=(steps,),
            in_specs=spec_blocks,
            out_specs=[pl.BlockSpec((2, 2, 2, piece // 2, LANES), lambda i, place: (0, 0, 0, i, 0))] * len(which),
        ),
        out_shape=[jax.ShapeDtypeStruct((2, 2, 2, size // 2, LANES), jnp.bfloat16)] * len(which),
        compiler_params=pltpu.CompilerParams(vmem_limit_bytes=56 * MIB),
        name="spectrum",
    )(place, *[spectrum] * len(which))


def four_real(a0, a1, a2, a3):
    even, odd = a0 + a2, a1 + a3
    less, more = (a1 - a3) * ROOT, odd * ROOT
    return (
        (even + odd, None),
        (a0 + less, -(a2 + more)),
        (a0 - a2, a3 - a1),
        (a0 - less, a2 - more),
        (even - odd, None),
    )


def residues_of(values, sign):
    even = four_real(*values[0::2])
    odd = four_real(*[v * sign for v in values[1::2]])
    out = [None] * SEQ
    out[0] = (even[0][0] + odd[0][0], None)
    out[4] = (even[4][0], -odd[4][0])
    for j in (1, 2, 3):
        turned = times(odd[j], root_16(-j))
        out[j] = (even[j][0] + turned[0], even[j][1] + turned[1])
        out[8 - j] = (even[j][0] - turned[0], turned[1] - even[j][1])
    return out


def four_back(zero, four, one, two, three):
    plus, minus = zero + four, zero - four
    half_way = (one[0] - three[0]) * ROOT
    across = (one[1] + three[1]) * ROOT
    return (
        plus + two[0] + (one[0] + three[0]),
        minus - two[1] + (half_way - across),
        plus - two[0] + (three[1] - one[1]),
        minus + two[1] - (half_way + across),
    )


def blocks_of(parts):
    sums, turned = [], []
    for j in (1, 2, 3):
        a, b = parts[j], parts[8 - j]
        sums.append((a[0] + b[0], a[1] - b[1]))
        turned.append(times((a[0] - b[0], a[1] + b[1]), root_16(j)))
    even = four_back(parts[0][0], parts[4][0], *sums)
    odd = four_back(parts[0][0], -parts[4][1], *turned)
    return [value for pair in zip(even, odd) for value in pair]


def sign_of_half():
    return jnp.where(lax.axis_index("seq") < HALF, 1.0, -1.0).astype(jnp.float32)


def turn_table(size):
    angles = np.arange(2 * SEQ)[:, None] * np.arange(size)[None, :] * (2.0 * np.pi / (2 * SEQ * size))
    angles = angles.reshape(2, SEQ, size)
    between = np.broadcast_to(np.arange(size) * (2.0 * np.pi / size), (2, 1, size))
    angles = np.concatenate([angles, between], axis=1)
    table = np.stack([np.cos(angles), np.sin(angles)], axis=2).astype(np.float32)
    return jnp.asarray(np.repeat(table[..., None], LANES, axis=-1))


def split_table(size):
    turns = np.arange(2 * SEQ).reshape(2, SEQ) / (2 * SEQ * size)
    turns = 2 * np.pi * np.concatenate([turns, np.full((2, 1), 1 / size)], axis=1)
    near, far = (turns[:, :, None] * tokens for tokens in (np.arange(NEAR), np.arange(0, size, NEAR)))
    near = np.repeat(np.stack([np.cos(near), np.sin(near)], axis=2)[..., None], LANES, axis=-1)
    far = np.stack([np.cos(far), np.sin(far)], axis=3).reshape(-1)
    return jnp.asarray(near, jnp.float32), jnp.asarray(far, jnp.float32)


def forward_kernel(tokens, near, far, dft_ref, re_ref, im_ref, stage):
    half = lax.axis_index("seq") // HALF
    sign = sign_of_half()
    size = tokens.shape[1]
    short = size // 2
    chunks = NEAR // STEP

    def twiddle(j, a, at):
        index = ((half * (SEQ + 1) + j) * (size // NEAR) + a) * 2
        return times((near[j, 0, at, :], near[j, 1, at, :]), (far[index], far[index + 1]))

    def rows_of(index, carry):
        a = index // chunks
        near_at = rows_at(index % chunks)
        both = []
        for late in range(2):
            at = rows_at(index, late * short)
            parts = residues_of([tokens[p, at, :].astype(jnp.float32) for p in range(SEQ)], sign)
            turned = []
            for j, (real, imag) in enumerate(parts):
                cos, sin = twiddle(j, a + late * (short // NEAR), near_at)
                if imag is None:
                    turned.append((real * cos, -(real * sin)))
                else:
                    turned.append((real * cos + imag * sin, imag * cos - real * sin))
            both.append(turned)
        at = rows_at(index)
        cos, sin = twiddle(SEQ, a, near_at)
        for j in range(SEQ):
            x, y = both[0][j], both[1][j]
            less = x[0] - y[0], x[1] - y[1]
            pair = (x[0] + y[0], x[1] + y[1]), (less[0] * cos + less[1] * sin, less[1] * cos - less[0] * sin)
            for bit, (real, imag) in enumerate(pair):
                to = pl.ds((bit * SEQ + j) * LANES, LANES)
                real = real.astype(jnp.bfloat16)
                stage[at, to] = real
                stage[rows_at(index, short), to] = imag.astype(jnp.bfloat16)
                stage[rows_at(index, size), to] = -real
        return carry

    lax.fori_loop(0, short // STEP, rows_of, 0, unroll=2)
    re_ref[...] = jnp.dot(dft_ref[...], stage[pl.ds(0, size), :], preferred_element_type=jnp.float32)
    im_ref[...] = jnp.dot(dft_ref[...], stage[pl.ds(short, size), :], preferred_element_type=jnp.float32)


def filter_members(members, spec, re_ref, im_ref, dft_ref, back_re, back_im, stage):
    place = lax.axis_index("seq") % HALF
    short = re_ref.shape[0]
    size = 2 * short
    for index, member in enumerate(members):
        for odd in range(2):
            for bit in range(2):
                column = bit * SEQ + 2 * (place ^ member) + odd
                at = pl.ds(pl.multiple_of(column * LANES, LANES), LANES)
                h = spec[index][0, odd, bit].astype(jnp.float32), spec[index][1, odd, bit].astype(jnp.float32)
                y_re, y_im = times((re_ref[:, at], im_ref[:, at]), h)
                y_re, y_im = y_re.astype(jnp.bfloat16), y_im.astype(jnp.bfloat16)
                to = pl.ds((odd * 2 + bit) * LANES, LANES)
                stage[index, pl.ds(0, short), to] = y_im
                stage[index, pl.ds(short, short), to] = y_re
                stage[index, pl.ds(size, short), to] = -y_im
        back_im[place ^ member] = jnp.dot(
            dft_ref[...], stage[index, pl.ds(0, size), :], preferred_element_type=jnp.float32
        )
        back_re[place ^ member] = jnp.dot(
            dft_ref[...], stage[index, pl.ds(short, size), :], preferred_element_type=jnp.float32
        )


def early_kernel(*refs):
    spec, (re_ref, im_ref, dft_ref, back_re, back_im, stage) = refs[: len(EARLY)], refs[len(EARLY) :]
    filter_members(EARLY, spec, re_ref, im_ref, dft_ref, back_re, back_im, stage)


def late_kernel(*refs):
    spec, refs = refs[: len(LATE)], refs[len(LATE) :]
    early_re, early_im, re_ref, im_ref, table, dft_ref, out_ref, back_re, back_im, stage = refs
    sign = sign_of_half()
    place = lax.axis_index("seq") % HALF
    short = re_ref.shape[0]
    size = 2 * short
    filter_members(LATE, spec, re_ref, im_ref, dft_ref, back_re, back_im, stage)
    scale = 1.0 / (2 * SEQ * size)

    def rows_of(index, carry, last):
        at = rows_at(index)
        late = rows_at(index, short)
        cos, sin = table[SEQ, 0, at, :], table[SEQ, 1, at, :]
        parts = [], []
        for j in range(SEQ):
            pair = []
            for bit in range(2):
                to = pl.ds((j % 2 * 2 + bit) * LANES, LANES)
                pair.append(tuple(ref[j // 2, at, to] for ref in ((back_re, back_im) if j // 2 == last else (early_re, early_im))))
            a, b = pair[0], times(pair[1], (cos, sin))
            parts[0].append(times((a[0] + b[0], a[1] + b[1]), (table[j, 0, at, :], table[j, 1, at, :])))
            parts[1].append(times((a[0] - b[0], a[1] - b[1]), (table[j, 0, late, :], table[j, 1, late, :])))
        for where, values in zip((at, late), parts):
            for p, value in enumerate(blocks_of(values)):
                out_ref[p, where, :] = (value * (scale * sign if p % 2 else scale)).astype(jnp.bfloat16)
        return carry

    for own in range(HALF):

        @pl.when(place == own)
        def _(last=own ^ LATE[0]):
            lax.fori_loop(0, short // STEP, functools.partial(rows_of, last=last), 0, unroll=2)


def table_kernel(member, table_hbm, near_hbm, key_ref, value_ref, skip_ref, table, near, out_ref, direct, held, sems):
    half = lax.axis_index("seq") // HALF
    copies = [
        pltpu.make_async_copy(source.at[half], to, sems.at[index])
        for index, (source, to) in enumerate(((table_hbm, table), (near_hbm, near)))
    ]
    for copy in copies:
        copy.start()
    for ch in range(CH):
        width = key_ref.shape[1] // CH
        at = pl.ds(ch * width, width)
        product = (key_ref[:, at].astype(jnp.float32) * value_ref[:, at].astype(jnp.float32)).astype(jnp.bfloat16)
        direct[:, at] = skip_ref[:, at] * product.astype(jnp.float32)
    rows = out_ref.shape[3]
    for part in range(2):
        for odd in range(2):
            held[...] = member[part, odd].astype(jnp.float32)
            for bit in range(2):
                out_ref[part, odd, bit] = held[pl.ds(bit, rows, stride=2), :].astype(jnp.bfloat16)
    for copy in copies:
        copy.wait()


def gate_kernel(gate_ref, direct, field_ref, out_hbm, held, sems):
    copies = []
    for ch in range(CH):
        for member in range(HALF):
            device = member * CH + ch
            at = columns_of(device)
            field = field_ref[device].astype(jnp.float32) + field_ref[device + DEVICES // 2].astype(jnp.float32)
            gated = gate_ref[:, at].astype(jnp.float32) * (field + direct[:, at])
            held[:, at] = gated.astype(jnp.bfloat16)
        columns = pl.ds(ch * HALF * LANES, HALF * LANES)
        copies.append(pltpu.make_async_copy(held.at[:, columns], out_hbm.at[:, columns], sems.at[ch]))
        copies[-1].start()
    for copy in copies:
        copy.wait()


def call(kernel, name, ins, outs, scratch=(), limit=24 * MIB, hbm=(), cost=None, aliases=None, to_hbm=False):
    return pl.pallas_call(
        kernel,
        out_shape=tuple(jax.ShapeDtypeStruct(shape, dtype) for shape, dtype in outs),
        in_specs=[pl.BlockSpec(memory_space=pl.ANY) if index in hbm else SMEM if x.ndim == 1 else VMEM for index, x in enumerate(ins)],
        out_specs=tuple(pl.BlockSpec(memory_space=pl.ANY) if to_hbm else VMEM for _ in outs),
        scratch_shapes=list(scratch),
        compiler_params=pltpu.CompilerParams(vmem_limit_bytes=limit),
        cost_estimate=cost,
        input_output_aliases=aliases or {},
        name=name,
    )(*ins)


def halves(gate_rows, key_rows, value_rows, spectrum, skip_bias):
    bf16, f32 = jnp.bfloat16, jnp.float32
    rows, channels = key_rows.shape
    size = rows * CH
    short = size // 2
    everywhere = ("seq", "ch")

    angles = np.arange(short)[:, None] * np.arange(short)[None, :] % short * (2.0 * np.pi / short)
    dft = jnp.asarray(np.concatenate([np.cos(angles), np.sin(angles)], axis=1), bf16)
    table = turn_table(size)
    near, far = split_table(size)

    sends = call(
        product_kernel,
        "product",
        [key_rows, value_rows],
        [((DEVICES, rows, LANES), bf16)],
        [pltpu.VMEM((rows, channels), bf16)] * 2 + [pltpu.SemaphoreType.DMA((2, CH))],
        limit=56 * MIB,
        hbm=(0, 1),
    )[0]
    opposite = lax.axis_index("seq") % HALF ^ 3
    last = lax.dynamic_slice_in_dim(spectrum, opposite * LANES, LANES, axis=3).astype(bf16)
    last = swap(last, "seq", 3, SEQ)
    cost = pl.CostEstimate(flops=40000000000, bytes_accessed=1 << 20, transcendentals=0)
    table, near, last, direct = call(
        table_kernel,
        "table",
        [last, table, near, key_rows, value_rows, skip_bias.reshape(1, channels)],
        [(table.shape[1:], f32), (near.shape[1:], f32), ((2, 2, 2, short, LANES), bf16), ((rows, channels), f32)],
        [pltpu.VMEM((size, LANES), f32), pltpu.SemaphoreType.DMA((2,))],
        hbm=(1, 2),
        cost=cost,
    )
    spec = members_of(spectrum, (0, 1, 2))
    tokens = lax.all_to_all(sends, everywhere, split_axis=0, concat_axis=0, tiled=True).reshape(SEQ, size, LANES)
    spec = [spec[0]] + [swap(spec[member], "seq", member, SEQ) for member in (1, 2)] + [last]
    freq = call(
        forward_kernel,
        "forward",
        [tokens, near, far, dft],
        [((short, 2 * SEQ * LANES), f32)] * 2,
        [pltpu.VMEM((3 * short, 2 * SEQ * LANES), bf16)],
    )
    back = ((HALF, short, 4 * LANES), f32)
    early = call(
        early_kernel,
        "early_members",
        [*[spec[member] for member in EARLY], *freq, dft],
        [back] * 2,
        [pltpu.VMEM((len(EARLY), 3 * short, 4 * LANES), bf16)],
    )
    shares = call(
        late_kernel,
        "late_member",
        [*[spec[member] for member in LATE], *early, *freq, table, dft],
        [((SEQ, size, LANES), bf16)],
        [pltpu.VMEM(*back)] * 2 + [pltpu.VMEM((len(LATE), 3 * short, 4 * LANES), bf16)],
    )[0].reshape(DEVICES, rows, LANES)
    field = lax.all_to_all(shares, everywhere, split_axis=0, concat_axis=0, tiled=True)
    return call(
        gate_kernel,
        "gate",
        [gate_rows, direct, field],
        [((rows, channels), bf16)],
        [pltpu.VMEM((rows, channels), bf16), pltpu.SemaphoreType.DMA((CH,))],
        to_hbm=True,
    )[0]


def solution(mesh):
    placed = (
        P(("seq", "ch"), None),
        P(("seq", "ch"), None),
        P(("seq", "ch"), None),
        P(None, "seq", None, "ch"),
        P(),
    )
    shape = dict(mesh.shape)
    body = halves if (shape["seq"], shape["ch"]) == (SEQ, CH) else any_mesh
    return jax.shard_map(
        body, mesh=mesh, in_specs=placed, out_specs=P(("seq", "ch"), None), check_vma=False
    )
```

```python
import functools
import math

import jax
import jax.numpy as jnp
import numpy as np
from jax import lax
from jax.experimental import pallas as pl
from jax.experimental.pallas import tpu as pltpu
from jax.sharding import PartitionSpec as P

highest = lax.Precision.HIGHEST
LANES = 128
MIB = 1 << 20


def phase_table(first, second, modulus):
    turns = first[:, None] * second[None, :] % modulus
    angles = turns.astype(jnp.float32) * (2.0 * math.pi / modulus)
    return (jnp.cos(angles), jnp.sin(angles))


def convolve(product, spectrum):
    seq_count = lax.axis_size("seq")
    tokens, width = product.shape
    length_two = 2 * seq_count * tokens
    offsets = jnp.arange(2 * seq_count, dtype=jnp.int32)
    places = jnp.arange(seq_count, dtype=jnp.int32)
    residues = jnp.arange(tokens, dtype=jnp.int32)
    off_cos, off_sin = phase_table(offsets, places, 2 * seq_count)
    res_cos, res_sin = phase_table(residues, residues, tokens)
    block = tokens // seq_count
    device = lax.axis_index("seq")
    pieces = lax.all_to_all(
        product.reshape(1, tokens, width), "seq", split_axis=1, concat_axis=0, tiled=True
    )
    values = pieces.astype(jnp.float32)
    real_part = jnp.einsum("kp,prc->krc", off_cos, values, precision=highest)
    imag_part = -jnp.einsum("kp,prc->krc", off_sin, values, precision=highest)
    own_rows = device * block + jnp.arange(block, dtype=jnp.int32)
    tw_cos, tw_sin = phase_table(offsets, own_rows, length_two)
    tw_cos = tw_cos[:, :, None]
    tw_sin = tw_sin[:, :, None]
    real_part, imag_part = (
        real_part * tw_cos + imag_part * tw_sin,
        imag_part * tw_cos - real_part * tw_sin,
    )
    real_part, imag_part = (
        lax.all_to_all(real_part, "seq", split_axis=0, concat_axis=1, tiled=True),
        lax.all_to_all(imag_part, "seq", split_axis=0, concat_axis=1, tiled=True),
    )
    real_next = jnp.einsum("grc,rs->gsc", real_part, res_cos, precision=highest) + jnp.einsum(
        "grc,rs->gsc", imag_part, res_sin, precision=highest
    )
    imag_next = jnp.einsum("grc,rs->gsc", imag_part, res_cos, precision=highest) - jnp.einsum(
        "grc,rs->gsc", real_part, res_sin, precision=highest
    )
    spec_real = spectrum[0]
    spec_imag = spectrum[1]
    real_part = real_next * spec_real - imag_next * spec_imag
    imag_part = real_next * spec_imag + imag_next * spec_real
    real_next = jnp.einsum("gsc,sr->grc", real_part, res_cos, precision=highest) - jnp.einsum(
        "gsc,sr->grc", imag_part, res_sin, precision=highest
    )
    imag_next = jnp.einsum("gsc,sr->grc", imag_part, res_cos, precision=highest) + jnp.einsum(
        "gsc,sr->grc", real_part, res_sin, precision=highest
    )
    own_offsets = 2 * device + jnp.arange(2, dtype=jnp.int32)
    un_cos, un_sin = phase_table(own_offsets, residues, length_two)
    un_cos = un_cos[:, :, None]
    un_sin = un_sin[:, :, None]
    real_part = real_next * un_cos - imag_next * un_sin
    imag_part = imag_next * un_cos + real_next * un_sin
    real_part, imag_part = (
        lax.all_to_all(real_part, "seq", split_axis=1, concat_axis=0, tiled=True),
        lax.all_to_all(imag_part, "seq", split_axis=1, concat_axis=0, tiled=True),
    )
    field = jnp.einsum("kp,krc->prc", off_cos, real_part, precision=highest) - jnp.einsum(
        "kp,krc->prc", off_sin, imag_part, precision=highest
    )
    field = field / length_two
    field = lax.all_to_all(field, "seq", split_axis=0, concat_axis=1, tiled=True)
    return field.reshape(tokens, width)


def any_mesh(gate_rows, key_rows, value_rows, spectrum, skip_bias):
    own = (key_rows.astype(jnp.float32) * value_rows.astype(jnp.float32)).astype(jnp.bfloat16)
    product = lax.all_to_all(own, "ch", split_axis=1, concat_axis=0, tiled=True)
    field = convolve(product, spectrum)
    field = lax.all_to_all(field, "ch", split_axis=0, concat_axis=1, tiled=True)
    gated = gate_rows.astype(jnp.float32) * (
        field + skip_bias[None, :] * own.astype(jnp.float32)
    )
    return gated.astype(jnp.bfloat16)


SEQ, CH, HALF = 8, 4, 4
DEVICES = SEQ * CH
ROOT = math.sqrt(0.5)
EARLY, LATE = (0, 1, 3), (2,)
NEAR = 64
VMEM = pl.BlockSpec(memory_space=pltpu.VMEM)
SMEM = pl.BlockSpec(memory_space=pltpu.SMEM)
STEP = 16


def swap(array, axis, mask, count):
    return lax.ppermute(array, axis, [(i, i ^ mask) for i in range(count)])


def columns_of(device):
    seq, ch = divmod(device, CH)
    return pl.ds((ch * HALF + seq % HALF) * LANES, LANES)


def rows_at(index, first=0):
    return pl.ds(pl.multiple_of(first + index * STEP, STEP), STEP)


def times(a, b):
    return a[0] * b[0] - a[1] * b[1], a[0] * b[1] + a[1] * b[0]


def root_16(power):
    return math.cos(power * math.pi / 8), math.sin(power * math.pi / 8)


def product_kernel(key_hbm, value_hbm, out_ref, key, value, sems):
    groups = DEVICES // 2
    width = key.shape[1] // CH
    copies = []
    for ch in range(CH):
        at = pl.ds(ch * width, width)
        copies.append(
            [
                pltpu.make_async_copy(source.at[:, at], to.at[:, at], sems.at[which, ch])
                for which, (source, to) in enumerate(((key_hbm, key), (value_hbm, value)))
            ]
        )
        for copy in copies[-1]:
            copy.start()
    for ch in range(CH):
        for copy in copies[ch]:
            copy.wait()
        for member in range(HALF):
            device = member * CH + ch
            at = columns_of(device)
            product = (key[:, at].astype(jnp.float32) * value[:, at].astype(jnp.float32)).astype(jnp.bfloat16)
            out_ref[device] = product
            out_ref[device + groups] = product


def spectrum_kernel(place_ref, *refs):
    count = len(refs) // 2
    spec, members = refs[:count], refs[count:]
    rows = members[0].shape[3]
    for member in range(count):
        for part in range(2):
            for odd in range(2):
                for bit in range(2):
                    values = spec[member][part, odd, pl.ds(bit, rows, stride=2), :]
                    members[member][part, odd, bit] = values.astype(jnp.bfloat16)


def members_of(spectrum, which, steps=4):
    size = spectrum.shape[2]
    piece = size // steps
    place = (lax.axis_index("seq") % HALF).astype(jnp.int32).reshape(1)
    spec_blocks = [
        pl.BlockSpec((2, 2, piece, LANES), lambda i, place, member=member: (0, 0, i, place[0] ^ member))
        for member in which
    ]
    return pl.pallas_call(
        spectrum_kernel,
        grid_spec=pltpu.PrefetchScalarGridSpec(
            num_scalar_prefetch=1,
            grid=(steps,),
            in_specs=spec_blocks,
            out_specs=[pl.BlockSpec((2, 2, 2, piece // 2, LANES), lambda i, place: (0, 0, 0, i, 0))] * len(which),
        ),
        out_shape=[jax.ShapeDtypeStruct((2, 2, 2, size // 2, LANES), jnp.bfloat16)] * len(which),
        compiler_params=pltpu.CompilerParams(vmem_limit_bytes=56 * MIB),
        name="spectrum",
    )(place, *[spectrum] * len(which))


def four_real(a0, a1, a2, a3):
    even, odd = a0 + a2, a1 + a3
    less, more = (a1 - a3) * ROOT, odd * ROOT
    return (
        (even + odd, None),
        (a0 + less, -(a2 + more)),
        (a0 - a2, a3 - a1),
        (a0 - less, a2 - more),
        (even - odd, None),
    )


def residues_of(values, sign):
    even = four_real(*values[0::2])
    odd = four_real(*[v * sign for v in values[1::2]])
    out = [None] * SEQ
    out[0] = (even[0][0] + odd[0][0], None)
    out[4] = (even[4][0], -odd[4][0])
    for j in (1, 2, 3):
        turned = times(odd[j], root_16(-j))
        out[j] = (even[j][0] + turned[0], even[j][1] + turned[1])
        out[8 - j] = (even[j][0] - turned[0], turned[1] - even[j][1])
    return out


def four_back(zero, four, one, two, three):
    plus, minus = zero + four, zero - four
    half_way = (one[0] - three[0]) * ROOT
    across = (one[1] + three[1]) * ROOT
    return (
        plus + two[0] + (one[0] + three[0]),
        minus - two[1] + (half_way - across),
        plus - two[0] + (three[1] - one[1]),
        minus + two[1] - (half_way + across),
    )


def blocks_of(parts):
    sums, turned = [], []
    for j in (1, 2, 3):
        a, b = parts[j], parts[8 - j]
        sums.append((a[0] + b[0], a[1] - b[1]))
        turned.append(times((a[0] - b[0], a[1] + b[1]), root_16(j)))
    even = four_back(parts[0][0], parts[4][0], *sums)
    odd = four_back(parts[0][0], -parts[4][1], *turned)
    return [value for pair in zip(even, odd) for value in pair]


def sign_of_half():
    return jnp.where(lax.axis_index("seq") < HALF, 1.0, -1.0).astype(jnp.float32)


def turn_table(size):
    angles = np.arange(2 * SEQ)[:, None] * np.arange(size)[None, :] * (2.0 * np.pi / (2 * SEQ * size))
    angles = angles.reshape(2, SEQ, size)
    between = np.broadcast_to(np.arange(size) * (2.0 * np.pi / size), (2, 1, size))
    angles = np.concatenate([angles, between], axis=1)
    table = np.stack([np.cos(angles), np.sin(angles)], axis=2).astype(np.float32)
    return jnp.asarray(np.repeat(table[..., None], LANES, axis=-1))


def split_table(size):
    turns = np.arange(2 * SEQ).reshape(2, SEQ) / (2 * SEQ * size)
    turns = 2 * np.pi * np.concatenate([turns, np.full((2, 1), 1 / size)], axis=1)
    near, far = (turns[:, :, None] * tokens for tokens in (np.arange(NEAR), np.arange(0, size, NEAR)))
    near = np.repeat(np.stack([np.cos(near), np.sin(near)], axis=2)[..., None], LANES, axis=-1)
    far = np.stack([np.cos(far), np.sin(far)], axis=3).reshape(-1)
    return jnp.asarray(near, jnp.float32), jnp.asarray(far, jnp.float32)


def forward_kernel(tokens, near, far, dft_ref, re_ref, im_ref, stage):
    half = lax.axis_index("seq") // HALF
    sign = sign_of_half()
    size = tokens.shape[1]
    short = size // 2
    chunks = NEAR // STEP

    def twiddle(j, a, at):
        index = ((half * (SEQ + 1) + j) * (size // NEAR) + a) * 2
        return times((near[j, 0, at, :], near[j, 1, at, :]), (far[index], far[index + 1]))

    def rows_of(index, carry):
        a = index // chunks
        near_at = rows_at(index % chunks)
        both = []
        for late in range(2):
            at = rows_at(index, late * short)
            parts = residues_of([tokens[p, at, :].astype(jnp.float32) for p in range(SEQ)], sign)
            turned = []
            for j, (real, imag) in enumerate(parts):
                cos, sin = twiddle(j, a + late * (short // NEAR), near_at)
                if imag is None:
                    turned.append((real * cos, -(real * sin)))
                else:
                    turned.append((real * cos + imag * sin, imag * cos - real * sin))
            both.append(turned)
        at = rows_at(index)
        cos, sin = twiddle(SEQ, a, near_at)
        for j in range(SEQ):
            x, y = both[0][j], both[1][j]
            less = x[0] - y[0], x[1] - y[1]
            pair = (x[0] + y[0], x[1] + y[1]), (less[0] * cos + less[1] * sin, less[1] * cos - less[0] * sin)
            for bit, (real, imag) in enumerate(pair):
                to = pl.ds((bit * SEQ + j) * LANES, LANES)
                real = real.astype(jnp.bfloat16)
                stage[at, to] = real
                stage[rows_at(index, short), to] = imag.astype(jnp.bfloat16)
                stage[rows_at(index, size), to] = -real
        return carry

    lax.fori_loop(0, short // STEP, rows_of, 0, unroll=2)
    re_ref[...] = jnp.dot(dft_ref[...], stage[pl.ds(0, size), :], preferred_element_type=jnp.float32)
    im_ref[...] = jnp.dot(dft_ref[...], stage[pl.ds(short, size), :], preferred_element_type=jnp.float32)


def filter_members(members, spec, re_ref, im_ref, dft_ref, back_re, back_im, stage):
    place = lax.axis_index("seq") % HALF
    short = re_ref.shape[0]
    size = 2 * short
    for index, member in enumerate(members):
        for odd in range(2):
            for bit in range(2):
                column = bit * SEQ + 2 * (place ^ member) + odd
                at = pl.ds(pl.multiple_of(column * LANES, LANES), LANES)
                h = spec[index][0, odd, bit].astype(jnp.float32), spec[index][1, odd, bit].astype(jnp.float32)
                y_re, y_im = times((re_ref[:, at], im_ref[:, at]), h)
                y_re, y_im = y_re.astype(jnp.bfloat16), y_im.astype(jnp.bfloat16)
                to = pl.ds((odd * 2 + bit) * LANES, LANES)
                beside = pl.ds((4 + odd * 2 + bit) * LANES, LANES)
                stage[index, pl.ds(0, short), to] = y_im
                stage[index, pl.ds(short, short), to] = y_re
                stage[index, pl.ds(0, short), beside] = y_re
                stage[index, pl.ds(short, short), beside] = -y_im
        both = jnp.dot(dft_ref[...], stage[index], preferred_element_type=jnp.float32)
        back_im[place ^ member] = both[:, : 4 * LANES]
        back_re[place ^ member] = both[:, 4 * LANES :]


def early_kernel(*refs):
    spec, (re_ref, im_ref, dft_ref, back_re, back_im, stage) = refs[: len(EARLY)], refs[len(EARLY) :]
    filter_members(EARLY, spec, re_ref, im_ref, dft_ref, back_re, back_im, stage)


def late_kernel(*refs):
    spec, refs = refs[: len(LATE)], refs[len(LATE) :]
    early_re, early_im, re_ref, im_ref, table, dft_ref, out_ref, back_re, back_im, stage = refs
    sign = sign_of_half()
    place = lax.axis_index("seq") % HALF
    short = re_ref.shape[0]
    size = 2 * short
    filter_members(LATE, spec, re_ref, im_ref, dft_ref, back_re, back_im, stage)
    scale = 1.0 / (2 * SEQ * size)

    def rows_of(index, carry, last):
        at = rows_at(index)
        late = rows_at(index, short)
        cos, sin = table[SEQ, 0, at, :], table[SEQ, 1, at, :]
        parts = [], []
        for j in range(SEQ):
            pair = []
            for bit in range(2):
                to = pl.ds((j % 2 * 2 + bit) * LANES, LANES)
                pair.append(tuple(ref[j // 2, at, to] for ref in ((back_re, back_im) if j // 2 == last else (early_re, early_im))))
            a, b = pair[0], times(pair[1], (cos, sin))
            parts[0].append(times((a[0] + b[0], a[1] + b[1]), (table[j, 0, at, :], table[j, 1, at, :])))
            parts[1].append(times((a[0] - b[0], a[1] - b[1]), (table[j, 0, late, :], table[j, 1, late, :])))
        for where, values in zip((at, late), parts):
            for p, value in enumerate(blocks_of(values)):
                out_ref[p, where, :] = (value * (scale * sign if p % 2 else scale)).astype(jnp.bfloat16)
        return carry

    for own in range(HALF):

        @pl.when(place == own)
        def _(last=own ^ LATE[0]):
            lax.fori_loop(0, short // STEP, functools.partial(rows_of, last=last), 0, unroll=2)


def table_kernel(member, table_hbm, near_hbm, key_ref, value_ref, skip_ref, table, near, out_ref, direct, held, sems):
    half = lax.axis_index("seq") // HALF
    copies = [
        pltpu.make_async_copy(source.at[half], to, sems.at[index])
        for index, (source, to) in enumerate(((table_hbm, table), (near_hbm, near)))
    ]
    for copy in copies:
        copy.start()
    for ch in range(CH):
        width = key_ref.shape[1] // CH
        at = pl.ds(ch * width, width)
        product = (key_ref[:, at].astype(jnp.float32) * value_ref[:, at].astype(jnp.float32)).astype(jnp.bfloat16)
        direct[:, at] = skip_ref[:, at] * product.astype(jnp.float32)
    rows = out_ref.shape[3]
    for part in range(2):
        for odd in range(2):
            held[...] = member[part, odd].astype(jnp.float32)
            for bit in range(2):
                out_ref[part, odd, bit] = held[pl.ds(bit, rows, stride=2), :].astype(jnp.bfloat16)
    for copy in copies:
        copy.wait()


def gate_kernel(gate_ref, direct, field_ref, out_hbm, held, sems):
    copies = []
    for ch in range(CH):
        for member in range(HALF):
            device = member * CH + ch
            at = columns_of(device)
            field = field_ref[device].astype(jnp.float32) + field_ref[device + DEVICES // 2].astype(jnp.float32)
            gated = gate_ref[:, at].astype(jnp.float32) * (field + direct[:, at])
            held[:, at] = gated.astype(jnp.bfloat16)
        columns = pl.ds(ch * HALF * LANES, HALF * LANES)
        copies.append(pltpu.make_async_copy(held.at[:, columns], out_hbm.at[:, columns], sems.at[ch]))
        copies[-1].start()
    for copy in copies:
        copy.wait()


def call(kernel, name, ins, outs, scratch=(), limit=24 * MIB, hbm=(), cost=None, aliases=None, to_hbm=False):
    return pl.pallas_call(
        kernel,
        out_shape=tuple(jax.ShapeDtypeStruct(shape, dtype) for shape, dtype in outs),
        in_specs=[pl.BlockSpec(memory_space=pl.ANY) if index in hbm else SMEM if x.ndim == 1 else VMEM for index, x in enumerate(ins)],
        out_specs=tuple(pl.BlockSpec(memory_space=pl.ANY) if to_hbm else VMEM for _ in outs),
        scratch_shapes=list(scratch),
        compiler_params=pltpu.CompilerParams(vmem_limit_bytes=limit),
        cost_estimate=cost,
        input_output_aliases=aliases or {},
        name=name,
    )(*ins)


def halves(gate_rows, key_rows, value_rows, spectrum, skip_bias):
    bf16, f32 = jnp.bfloat16, jnp.float32
    rows, channels = key_rows.shape
    size = rows * CH
    short = size // 2
    everywhere = ("seq", "ch")

    angles = np.arange(short)[:, None] * np.arange(short)[None, :] % short * (2.0 * np.pi / short)
    dft = jnp.asarray(np.concatenate([np.cos(angles), np.sin(angles)], axis=1), bf16)
    table = turn_table(size)
    near, far = split_table(size)

    sends = call(
        product_kernel,
        "product",
        [key_rows, value_rows],
        [((DEVICES, rows, LANES), bf16)],
        [pltpu.VMEM((rows, channels), bf16)] * 2 + [pltpu.SemaphoreType.DMA((2, CH))],
        limit=56 * MIB,
        hbm=(0, 1),
    )[0]
    opposite = lax.axis_index("seq") % HALF ^ 3
    last = lax.dynamic_slice_in_dim(spectrum, opposite * LANES, LANES, axis=3).astype(bf16)
    last = swap(last, "seq", 3, SEQ)
    cost = pl.CostEstimate(flops=40000000000, bytes_accessed=1 << 20, transcendentals=0)
    table, near, last, direct = call(
        table_kernel,
        "table",
        [last, table, near, key_rows, value_rows, skip_bias.reshape(1, channels)],
        [(table.shape[1:], f32), (near.shape[1:], f32), ((2, 2, 2, short, LANES), bf16), ((rows, channels), f32)],
        [pltpu.VMEM((size, LANES), f32), pltpu.SemaphoreType.DMA((2,))],
        hbm=(1, 2),
        cost=cost,
    )
    spec = members_of(spectrum, (0, 1, 2))
    tokens = lax.all_to_all(sends, everywhere, split_axis=0, concat_axis=0, tiled=True).reshape(SEQ, size, LANES)
    spec = [spec[0]] + [swap(spec[member], "seq", member, SEQ) for member in (1, 2)] + [last]
    freq = call(
        forward_kernel,
        "forward",
        [tokens, near, far, dft],
        [((short, 2 * SEQ * LANES), f32)] * 2,
        [pltpu.VMEM((3 * short, 2 * SEQ * LANES), bf16)],
    )
    back = ((HALF, short, 4 * LANES), f32)
    early = call(
        early_kernel,
        "early_members",
        [*[spec[member] for member in EARLY], *freq, dft],
        [back] * 2,
        [pltpu.VMEM((len(EARLY), 2 * short, 8 * LANES), bf16)],
    )
    shares = call(
        late_kernel,
        "late_member",
        [*[spec[member] for member in LATE], *early, *freq, table, dft],
        [((SEQ, size, LANES), bf16)],
        [pltpu.VMEM(*back)] * 2 + [pltpu.VMEM((len(LATE), 2 * short, 8 * LANES), bf16)],
    )[0].reshape(DEVICES, rows, LANES)
    field = lax.all_to_all(shares, everywhere, split_axis=0, concat_axis=0, tiled=True)
    return call(
        gate_kernel,
        "gate",
        [gate_rows, direct, field],
        [((rows, channels), bf16)],
        [pltpu.VMEM((rows, channels), bf16), pltpu.SemaphoreType.DMA((CH,))],
        to_hbm=True,
    )[0]


def solution(mesh):
    placed = (
        P(("seq", "ch"), None),
        P(("seq", "ch"), None),
        P(("seq", "ch"), None),
        P(None, "seq", None, "ch"),
        P(),
    )
    shape = dict(mesh.shape)
    body = halves if (shape["seq"], shape["ch"]) == (SEQ, CH) else any_mesh
    return jax.shard_map(
        body, mesh=mesh, in_specs=placed, out_specs=P(("seq", "ch"), None), check_vma=False
    )
```
